256 devices in a mesh: tm: 8 (over y, x_hi), space: 32 (over z, x_lo, core).
Axes of the slice: x: 4 (x_hi: 2, x_lo: 2; x = x_hi * 2 + x_lo), y: 4, z: 8, core: 2. Of those that a mesh axis runs over, the one named last changes fastest.
Arguments:
- starts: float32 [8, 3, 256, 32, 128], P('tm', None, 'space'), may hold values from -6 to 6
- source: float32 [8, 3, 256, 32, 128], P('tm', None, 'space'), may hold values from -6 to 6
- mass_term: float32 [256, 32, 128], P('space'), may hold values from 0.5 to 4
- curve_entry: int32 [256, 32, 128], P('space'), may hold values from 0 to 63
- curve_table: float32 [2, 64], replicated, may hold values from 0.3 to 3
Outputs:
- next_starts: float32 [8, 3, 256, 32, 128], P('tm', None, 'space')
The draws below stay inside these ranges and needn't reach their ends.
All inputs are finite; a program needn't handle non-finite values.
Results may differ from the reference program's by a relative error of at most 0.00002.
Values sent between devices are 32-bit elements; how exact they have to be, the bound alone decides.
A program may use at most 64 MiB of HBM per device.

```python
import math
import jax
import jax.numpy as jnp

NY = 32
NX = 128
TBL = 64
STEPS = 2
UPDATES = 2
SWEEPS = 4
C_SWEEPS = 2
NT = 8
NZ = 256


def draw_starts(key, part):
    key = jax.random.fold_in(key, 5)
    shape = (NT, 3, NZ, NY, NX)
    return jnp.clip(jax.random.normal(key, shape, jnp.float32), -6.0, 6.0)


def draw_source(key, part):
    key = jax.random.fold_in(key, 7)
    shape = (NT, 3, NZ, NY, NX)
    return jnp.clip(jax.random.normal(key, shape, jnp.float32), -6.0, 6.0)


def place_ends(drawn, stream_key, smallest, top_value):
    place = [jax.random.randint(jax.random.fold_in(stream_key, axis), (), 0, length) for axis, length in enumerate(drawn.shape)]
    widest = drawn.shape.index(max(drawn.shape))
    neighbour = place[:widest] + [(place[widest] + 1) % drawn.shape[widest]] + place[widest + 1:]
    return drawn.at[tuple(place)].set(smallest).at[tuple(neighbour)].set(top_value)


def block_levels(rng, shape, cuts, least, high):
    loudness, own = 1.0, jax.random.fold_in(rng, 6)
    for position, blocks in cuts:
        heights = jnp.exp(jax.random.uniform(jax.random.fold_in(own, position), (blocks,), jnp.float32, least / len(cuts), high / len(cuts)))
        loudness = loudness * jnp.repeat(heights, shape[position] // blocks).reshape([-1 if axis == position else 1 for axis in range(len(shape))])
    return loudness


def setup_inputs(seed: int = 0) -> dict:
    arg_keys = jax.random.split(jax.random.key(seed), 6)
    return {
        "starts": draw_starts(jax.random.fold_in(arg_keys[5], 71), 0),
        "source": draw_source(jax.random.fold_in(arg_keys[5], 71), 0),
        "mass_term": jnp.clip(jnp.exp(math.log(4.0) - 2.0794415 * jax.random.uniform(arg_keys[2], (NZ, NY, NX), jnp.float32) ** block_levels(arg_keys[2], (NZ, NY, NX), ((0, 32),), -0.2, 0.2)), 0.5, 4.0),
        "curve_entry": place_ends(jax.random.randint(arg_keys[3], (NZ, NY, NX), 0, TBL), jax.random.fold_in(arg_keys[3], 1), 0, TBL - 1).astype(jnp.int32),
        "curve_table": jnp.clip(jnp.exp(jax.random.uniform(arg_keys[4], (2, TBL), jnp.float32, math.log(0.3), math.log(3.0))), 0.3, 3.0),
    }


relaxation = 0.45


def upper_planes(potential):
    return jnp.concatenate([potential[:, 1:], jnp.zeros_like(potential[:, :1])], axis=1)


def curl_forward(potential, shifted):
    along_z = shifted - potential
    along_y = jnp.roll(potential, -1, -2) - potential
    along_x = jnp.roll(potential, -1, -1) - potential
    return jnp.stack([along_y[2] - along_z[1], along_z[0] - along_x[2], along_x[1] - along_y[0]])


def curl_adjoint(intensity, lower_plane):
    before = jnp.concatenate([lower_plane[:, None], intensity[:, :-1]], axis=1)
    along_z = before - intensity
    along_y = jnp.roll(intensity, 1, -2) - intensity
    along_x = jnp.roll(intensity, 1, -1) - intensity
    return jnp.stack([along_z[1] - along_y[2], along_x[2] - along_z[0], along_y[0] - along_x[1]])


def reluctance(induction, base_value, saturation):
    squared = induction[0] * induction[0] + induction[1] * induction[1] + induction[2] * induction[2]
    return base_value * (1.0 + saturation * squared / (1.0 + squared))


def diagonal(reluct_cell, lower_plane, mass_term):
    before_z = jnp.concatenate([lower_plane[None], reluct_cell[:-1]], axis=0)
    before_y = jnp.roll(reluct_cell, 1, -2)
    before_x = jnp.roll(reluct_cell, 1, -1)
    doubled = 2.0 * reluct_cell
    return jnp.stack([mass_term + doubled + before_z + before_y,
                      mass_term + doubled + before_z + before_x,
                      mass_term + doubled + before_y + before_x])


def frozen_update(initial, right_side, mass_term, sweeps, base_value, saturation):
    induction = curl_forward(initial, upper_planes(initial))
    reluct_cell = reluctance(induction, base_value, saturation)
    diagonal_terms = diagonal(reluct_cell, jnp.zeros_like(reluct_cell[0]), mass_term)
    potential = initial
    for sweep_index in range(sweeps):
        if sweep_index > 0:
            induction = curl_forward(potential, upper_planes(potential))
        intensity = reluct_cell[None] * induction
        operator_image = mass_term * potential + curl_adjoint(intensity, jnp.zeros_like(intensity[:, 0]))
        potential = potential + relaxation * (right_side - operator_image) / diagonal_terms
    return potential


def fine_map(initial, current, mass_term, base_value, saturation):
    potential = initial
    for step_index in range(STEPS):
        right_side = mass_term * potential + current
        for update_index in range(UPDATES):
            potential = frozen_update(potential, right_side, mass_term, SWEEPS, base_value, saturation)
    return potential


def coarse_map(initial, current, mass_term, base_value, saturation):
    coarse_mass = mass_term / STEPS
    return frozen_update(initial, coarse_mass * initial + current, coarse_mass, C_SWEEPS, base_value, saturation)


def reference(starts, source, mass_term, curve_entry, curve_table):
    base_value = curve_table[0][curve_entry]
    saturation = curve_table[1][curve_entry]
    corrections = []
    for interval in range(NT - 1):
        fine_end = fine_map(starts[interval], source[interval], mass_term, base_value, saturation)
        coarse_end = coarse_map(starts[interval], source[interval], mass_term, base_value, saturation)
        corrections.append(fine_end - coarse_end)
    running = fine_map(starts[NT - 1], source[NT - 1], mass_term, base_value, saturation)
    results = [running]
    for interval in range(NT - 1):
        running = coarse_map(running, source[interval], mass_term, base_value, saturation) + corrections[interval]
        results.append(running)
    return jnp.stack(results)
```

```python
import functools

import jax
import jax.numpy as jnp
from jax import lax
from jax.experimental import pallas as pl
from jax.experimental.pallas import tpu as pltpu
from jax.sharding import PartitionSpec as P

STEPS = 2
UPDATES = 2
SWEEPS = 4
RELAX = 0.45

Z, NY, NX = 8, 32, 128
PIECE = 4
PIECES = NY // PIECE
TBL = 64
SEND, RECV = 0, 1


def next_y(v):
    return pltpu.roll(v, v.shape[-2] - 1, v.ndim - 2)


def next_x(v):
    return pltpu.roll(v, v.shape[-1] - 1, v.ndim - 1)


def prev_y(v):
    return pltpu.roll(v, 1, v.ndim - 2)


def prev_x(v):
    return pltpu.roll(v, 1, v.ndim - 1)


def curl(v, above_x, above_y):
    x, y, z = v
    return (
        (next_y(z) - z) - (above_y - y),
        (above_x - x) - (next_x(z) - z),
        (next_x(y) - y) - (next_y(x) - x),
    )


def curl_adjoint(h, below_x, below_y):
    x, y, z = h
    return (
        (below_y - y) - (prev_y(z) - z),
        (prev_x(z) - z) - (below_x - x),
        (prev_y(x) - x) - (prev_x(y) - y),
    )


def reluctance(b, base, sat):
    squared = b[0] * b[0] + b[1] * b[1] + b[2] * b[2]
    return base * (1.0 + sat * squared / (1.0 + squared))


def step_sizes(mass, nu, below, relax):
    common = mass + 2.0 * nu
    before_y, before_x = prev_y(nu), prev_x(nu)
    return (
        relax / (common + below + before_y),
        relax / (common + below + before_x),
        relax / (common + before_y + before_x),
    )


def kernel(
    T, K,
    starts, source, mass, entry, table,
    out,
    X, XC, SRC, S, E, BASE, SAT, NU, W, R, H, PQ, V9, NUM, PQS, V9S,
    PS, CB, JS, JB, PB, SYU, SYD, YL, YH, ZL, ZH, OB,
    XW, MW, BW, SW, JW, CW, RW,
    lsem, isem, psem, vsem, nsem, csem, jsem, hsem, osem,
):
    t = lax.axis_index("tm")
    k = lax.axis_index("space")
    up, down = lax.rem(k + 1, K), lax.rem(k + K - 1, K)

    def piece_of(d):
        odd = lax.rem(d, 2)
        half = d // 2
        return half * (1 - odd) + (T - 1 - half) * odd

    def group_of(i):
        low = (i < T // 2).astype(jnp.int32) if not isinstance(i, int) else int(i < T // 2)
        return 2 * i * low + (2 * T - 1 - 2 * i) * (1 - low)

    me = piece_of(t)
    right = group_of(lax.rem(me + 1, T))
    left = group_of(lax.rem(me + T - 1, T))

    def remote(src, dst, send, recv, tm, space):
        return pltpu.make_async_remote_copy(
            src_ref=src, dst_ref=dst, send_sem=send, recv_sem=recv,
            device_id=(tm, space), device_id_type=pl.DeviceIdType.MESH,
        )

    loads = [
        pltpu.make_async_copy(starts, X.at[:, 2:10], lsem.at[0]),
        pltpu.make_async_copy(source, SRC.at[:, 1:9], lsem.at[1]),
        pltpu.make_async_copy(mass, S.at[1:9], lsem.at[2]),
        pltpu.make_async_copy(entry, E.at[2:10], lsem.at[3]),
    ]
    for load in loads:
        load.start()

    barrier = pltpu.get_barrier_semaphore()

    def greet(tm, space):
        pl.semaphore_signal(
            barrier, inc=1, device_id=(tm, space), device_id_type=pl.DeviceIdType.MESH
        )

    for space in (up, down):
        for tm in (t, left, right):
            greet(tm, space)
    for r in range(1, T):
        greet(lax.rem(t + r, T), k)
    pl.semaphore_wait(barrier, 6 + T - 1)

    first = [
        remote(starts.at[:, 6:8], X.at[:, 0:2], isem.at[0, 0], isem.at[1, 0], t, up),
        remote(starts.at[:, 0:2], X.at[:, 10:12], isem.at[0, 1], isem.at[1, 1], t, down),
        remote(entry.at[6:8], E.at[0:2], isem.at[0, 2], isem.at[1, 2], t, up),
        remote(entry.at[0:1], E.at[10:11], isem.at[0, 3], isem.at[1, 3], t, down),
        remote(mass.at[7:8], S.at[0:1], isem.at[0, 4], isem.at[1, 4], t, up),
        remote(mass.at[0:1], S.at[9:10], isem.at[0, 5], isem.at[1, 5], t, down),
        remote(source.at[:, 7:8], SRC.at[:, 0:1], isem.at[0, 6], isem.at[1, 6], t, up),
        remote(source.at[:, 0:1], SRC.at[:, 9:10], isem.at[0, 7], isem.at[1, 7], t, down),
    ]
    for copy in first:
        copy.start()

    keep_bottom = jnp.where(k > 0, 1.0, 0.0).astype(jnp.float32)
    keep_top = jnp.where(k < K - 1, 1.0, 0.0).astype(jnp.float32)

    def look_up(p):
        cells = E[p]

        def body(j, acc):
            hit = cells == j
            return jnp.where(hit, table[0, j], acc[0]), jnp.where(hit, table[1, j], acc[1])

        zeros = jnp.zeros((NY, NX), jnp.float32)
        b, s = lax.fori_loop(0, TBL, body, (zeros, zeros))
        BASE[p] = b
        SAT[p] = s

    def look_up_loop(lo, hi):
        def body(p, c):
            look_up(p)
            return c

        lax.fori_loop(lo, hi, body, 0)

    loads[3].wait()
    look_up_loop(2, 10)
    for load in loads[:3]:
        load.wait()
    first[2].wait_recv()
    first[3].wait_recv()
    look_up_loop(0, 2)
    look_up(10)
    BASE[0:2] = BASE[0:2] * keep_bottom
    for c in (0, 1, 4, 5, 6, 7):
        first[c].wait_recv()
    X[:, 10:12] = X[:, 10:12] * keep_top

    for c in range(3):
        def window(p, carry, c=c):
            v = SRC[c, p]
            even, odd = pltpu.roll(v, 2, 0), pltpu.roll(v, NY - 2, 0)
            for i in range(PIECES):
                JS[i, c, p] = (odd if i % 2 else even)[8 * (i // 2):8 * (i // 2) + 8]
            return carry

        lax.fori_loop(0, 10, window, 0)

    @pl.when(t < T - 1)
    def _():
        for r in range(1, T):
            d = lax.rem(t + r, T)
            remote(JS.at[piece_of(d)], JB.at[t], jsem.at[0, r], jsem.at[1, t], d, k).start()
        pltpu.make_async_copy(JS.at[me], JB.at[t], jsem.at[1, t]).start()

    def window_of(v):
        return pltpu.roll(v, lax.rem(2 * NY + 2 - PIECE * me, NY), 0)[0:8]

    for p in range(11):
        BW[p] = window_of(BASE[p])
        SW[p] = window_of(SAT[p])
    for p in range(10):
        MW[p] = window_of(S[p]) * (1.0 / STEPS)
        RW[p] = jnp.full((8, NX), RELAX, jnp.float32) * (keep_top if p == 9 else 1.0)

    def field(ref, z):
        return [ref[c, z + 2] for c in range(3)]

    V9[0] = X[0:2, 11]
    low = field(X, -2)
    PQ[0, 0] = next_y(low[2]) - low[2] + low[1]
    PQ[0, 1] = next_x(low[2]) - low[2] + low[0]
    b = curl(low, X[0, 1], X[1, 1])
    NU[0] = reluctance(b, BASE[0], SAT[0])

    def nu_at(z, above_x, above_y):
        NU[z + 2] = reluctance(curl(field(X, z), above_x, above_y), BASE[z + 2], SAT[z + 2])

    def w_at(z, scale):
        relax = RELAX * keep_top if z == Z else RELAX
        w = step_sizes(S[z + 1] * scale, NU[z + 2], NU[z + 1], relax)
        for c in range(3):
            W[c, z + 1] = w[c]

    def intensity(ref, z, above_x, above_y):
        b = curl(field(ref, z), above_x, above_y)
        nu = NU[z + 2]
        return [nu * b[0], nu * b[1], nu * b[2]]

    def low_intensity(ref, slot):
        nu = NU[0]
        return nu * (PQ[slot, 0] - ref[1, 1]), nu * (ref[0, 1] - PQ[slot, 1])

    for z in range(-1, Z):
        nu_at(z, X[0, z + 3], X[1, z + 3])
    nu_at(Z, V9[0, 0], V9[0, 1])
    for z in range(-1, Z + 1):
        w_at(z, 1.0 / STEPS)
    hx, hy = low_intensity(X, 0)
    for z in range(-1, Z + 1):
        h = intensity(X, z, X[0, z + 3], X[1, z + 3])
        a = curl_adjoint(h, hx, hy)
        for c in range(3):
            XC[c, z + 2] = X[c, z + 2] + W[c, z + 1] * (SRC[c, z + 1] - a[c])
        hx, hy = h[0], h[1]
    h = intensity(XC, -1, XC[0, 2], XC[1, 2])
    hx, hy = h[0], h[1]
    for z in range(Z):
        h = intensity(XC, z, XC[0, z + 3], XC[1, z + 3])
        a = curl_adjoint(h, hx, hy)
        for c in range(3):
            x = XC[c, z + 2]
            drift = (1.0 / STEPS) * S[z + 1] * (X[c, z + 2] - x)
            XC[c, z + 2] = x + W[c, z + 1] * (SRC[c, z + 1] + drift - a[c])
        hx, hy = h[0], h[1]

    total = STEPS * UPDATES * SWEEPS

    def up_copy(m):
        return remote(PQS.at[m], PQ.at[m], psem.at[0, m], psem.at[1, m], t, up)

    def down_copy(m):
        return remote(V9S.at[m], V9.at[m], vsem.at[0, m], vsem.at[1, m], t, down)

    def nu_copy(u):
        return remote(NUM.at[0, u], NUM.at[1, u], nsem.at[0, u], nsem.at[1, u], t, up)

    def relax_plane(z, h, hx, hy):
        a = curl_adjoint(h, hx, hy)
        s = S[z + 1]
        new = []
        for c in range(3):
            x = X[c, z + 2]
            new.append(x + W[c, z + 1] * (R[c, z + 1] - s * x - a[c]))
            X[c, z + 2] = new[c]
        return new

    def sweep(u, i):
        m = u * SWEEPS + i
        h = intensity(X, -1, X[0, 2], X[1, 2])
        for c in range(3):
            H[c] = h[c]
        hx, hy = h[0], h[1]
        for z in range(Z):
            h = intensity(X, z, X[0, z + 3], X[1, z + 3])
            new = relax_plane(z, h, hx, hy)
            hx, hy = h[0], h[1]
            if z == 1:
                @pl.when(m < total - 1)
                def _(new=new):
                    V9S[m + 1, 0] = new[0]
                    V9S[m + 1, 1] = new[1]
                    down_copy(m + 1).start()
            if z == Z - 2:
                @pl.when(m < total - 1)
                def _(new=new):
                    PQS[m + 1, 0] = next_y(new[2]) - new[2] + new[1]
                    PQS[m + 1, 1] = next_x(new[2]) - new[2] + new[0]
                    up_copy(m + 1).start()
        H[3] = hx
        H[4] = hy

        @pl.when(m > 0)
        def _():
            down_copy(m).wait_recv()
            up_copy(m).wait_recv()

        @pl.when(i == 0)
        def _():
            @pl.when(u > 0)
            def _():
                nu_copy(u).wait_recv()
                NU[0] = NUM[1, u] * keep_bottom

            nu_at(Z, V9[m, 0], V9[m, 1])
            w_at(Z, 1.0)
            w_at(-1, 1.0)

        h = intensity(X, Z, V9[m, 0], V9[m, 1])
        relax_plane(Z, h, H[3], H[4])
        hx, hy = low_intensity(X, m)
        relax_plane(-1, [H[0], H[1], H[2]], hx, hy)

    def update(u, carry):
        @pl.when(lax.rem(u, UPDATES) == 0)
        def _():
            for p in range(10):
                for c in range(3):
                    R[c, p] = S[p] * X[c, p + 1] + SRC[c, p]

        @pl.when(u > 0)
        def _():
            nu_at(Z - 2, X[0, Z + 1], X[1, Z + 1])
            NUM[0, u] = NU[Z]
            nu_copy(u).start()

        for z in range(-1, Z):
            nu_at(z, X[0, z + 3], X[1, z + 3])
        for z in range(Z):
            w_at(z, 1.0)

        def one(i, c):
            sweep(u, i)
            return c

        lax.fori_loop(0, SWEEPS, one, 0)
        return carry

    lax.fori_loop(0, STEPS * UPDATES, update, 0)

    is_correction = jnp.where(t < T - 1, 1.0, 0.0).astype(jnp.float32)

    def pieces(z, carry):
        for c in range(3):
            v = X[c, z + 2] - is_correction * XC[c, z + 2]
            for i in range(PIECES):
                PS[i, c, z] = v[PIECE * i:PIECE * i + PIECE]
        return carry

    lax.fori_loop(0, Z, pieces, 0)
    for r in range(1, T):
        d = lax.rem(t + r, T)
        remote(PS.at[piece_of(d)], CB.at[t], csem.at[0, r], csem.at[1, t], d, k).start()
    pltpu.make_async_copy(PS.at[me], CB.at[t], csem.at[1, t]).start()

    def arrived(ref, sem):
        pltpu.make_async_copy(ref, ref, sem).wait()

    arrived(CB.at[T - 1], csem.at[1, T - 1])
    for c in range(3):
        XW[c] = jnp.zeros((Z + 4, 8, NX), jnp.float32)
        CW[c] = jnp.zeros((Z, 8, NX), jnp.float32)
    for c in range(3):
        XW[c, 2:10, 2:6] = CB[T - 1, c]

    def out_remote(n):
        return remote(PB.at[n], OB.at[me], osem.at[0, n], osem.at[1, me], n, k)

    def emit(n):
        for c in range(3):
            PB[n, c] = XW[c, 2:10, 2:6]

        @pl.when(t != n)
        def _():
            out_remote(n).start()

        @pl.when(t == n)
        def _():
            pltpu.make_async_copy(PB.at[n], OB.at[me], osem.at[1, me]).start()

    def halos(n):
        s, r = hsem.at[0, n], hsem.at[1, n]
        return [
            remote(SYU.at[n], YL.at[n, :, 2:10], s.at[0], r.at[0], right, k),
            remote(SYD.at[n], YH.at[n, :, 2:10], s.at[1], r.at[1], left, k),
            remote(PB.at[n, :, 6:8], ZL.at[n], s.at[2], r.at[2], t, up),
            remote(PB.at[n, :, 0:2], ZH.at[n], s.at[3], r.at[3], t, down),
            remote(SYU.at[n, :, 6:8], YL.at[n, :, 0:2], s.at[4], r.at[4], right, up),
            remote(SYU.at[n, :, 0:2], YL.at[n, :, 10:12], s.at[5], r.at[5], right, down),
            remote(SYD.at[n, :, 6:8], YH.at[n, :, 0:2], s.at[6], r.at[6], left, up),
            remote(SYD.at[n, :, 0:2], YH.at[n, :, 10:12], s.at[7], r.at[7], left, down),
        ]

    def propagate(n, carry):
        for c in range(3):
            SYU[n, c] = XW[c, 2:10, 4:6]
            SYD[n, c] = XW[c, 2:10, 2:4]
        emit_first = halos(n)
        emit(n)
        for copy in emit_first:
            copy.start()
        arrived(JB.at[n], jsem.at[1, n])
        arrived(CB.at[n], csem.at[1, n])
        for c in range(3):
            CW[c, :, 2:6] = CB[n, c]
        for copy in emit_first:
            copy.wait_recv()
        for c in range(3):
            XW[c, :, 0:2] = YL[n, c]
            XW[c, :, 6:8] = YH[n, c]
            XW[c, 0:2, 2:6] = ZL[n, c]
            XW[c, 10:12, 2:6] = ZH[n, c]
            XW[c, 10:12] = XW[c, 10:12] * keep_top
        x0 = [XW[c] for c in range(3)]
        b = curl([v[:-1] for v in x0], x0[0][1:], x0[1][1:])
        nu = reluctance(b, BW[...], SW[...])
        h = [nu * v for v in b]
        w = step_sizes(MW[...], nu[1:], nu[:-1], RW[...])
        a = curl_adjoint([v[1:] for v in h], h[0][:-1], h[1][:-1])
        x1 = [x0[c][1:-1] + w[c] * (JB[n, c] - a[c]) for c in range(3)]
        b = curl([v[:-1] for v in x1], x1[0][1:], x1[1][1:])
        h = [nu[1:-1] * v for v in b]
        a = curl_adjoint([v[1:] for v in h], h[0][:-1], h[1][:-1])
        for c in range(3):
            x = x1[c][1:-1]
            drift = MW[1:9] * (x0[c][2:10] - x)
            x = x + w[c][1:-1] * (JB[n, c, 1:9] + drift - a[c])
            XW[c, 2:10] = x + CW[c]
        return carry

    lax.fori_loop(0, T - 1, propagate, 0)
    emit(T - 1)

    for i in range(PIECES):
        arrived(OB.at[i], osem.at[1, i])

    def place(z, carry):
        for c in range(3):
            for i in range(PIECES):
                out[c, z, PIECE * i:PIECE * i + PIECE] = OB[i, c, z]
        return carry

    lax.fori_loop(0, Z, place, 0)

    for copy in first:
        copy.wait_send()

    def sent(m, carry):
        up_copy(m).wait_send()
        down_copy(m).wait_send()
        return carry

    lax.fori_loop(1, total, sent, 0)
    for u in range(1, STEPS * UPDATES):
        nu_copy(u).wait_send()
    for r in range(1, T):
        d = lax.rem(t + r, T)
        remote(PS.at[piece_of(d)], CB.at[t], csem.at[0, r], csem.at[1, t], d, k).wait_send()

    @pl.when(t < T - 1)
    def _():
        for r in range(1, T):
            d = lax.rem(t + r, T)
            remote(JS.at[piece_of(d)], JB.at[t], jsem.at[0, r], jsem.at[1, t], d, k).wait_send()

    def halos_sent(n, carry):
        for copy in halos(n):
            copy.wait_send()
        return carry

    lax.fori_loop(0, T - 1, halos_sent, 0)

    def out_sent(n, carry):
        @pl.when(t != n)
        def _():
            out_remote(n).wait_send()

        return carry

    lax.fori_loop(0, T, out_sent, 0)


def body(mesh, starts, source, mass_term, curve_entry, curve_table):
    T, K = mesh.shape["tm"], mesh.shape["space"]
    total = STEPS * UPDATES * SWEEPS
    f32 = jnp.float32
    vm = lambda *shape: pltpu.VMEM(shape, f32)
    dma = lambda *shape: pltpu.SemaphoreType.DMA(shape)
    scratch = [
        vm(3, Z + 4, NY, NX),
        vm(3, Z + 4, NY, NX),
        vm(3, Z + 2, NY, NX),
        vm(Z + 2, NY, NX),
        pltpu.VMEM((Z + 3, NY, NX), jnp.int32),
        vm(Z + 3, NY, NX),
        vm(Z + 3, NY, NX),
        vm(Z + 3, NY, NX),
        vm(3, Z + 2, NY, NX),
        vm(3, Z + 2, NY, NX),
        vm(5, NY, NX),
        vm(total, 2, NY, NX),
        vm(total, 2, NY, NX),
        vm(2, STEPS * UPDATES, NY, NX),
        vm(total, 2, NY, NX),
        vm(total, 2, NY, NX),
        vm(PIECES, 3, Z, PIECE, NX),
        vm(T, 3, Z, PIECE, NX),
        vm(PIECES, 3, Z + 2, 8, NX),
        vm(T, 3, Z + 2, 8, NX),
        vm(T, 3, Z, PIECE, NX),
        vm(T, 3, Z, 2, NX),
        vm(T, 3, Z, 2, NX),
        vm(T, 3, Z + 4, 2, NX),
        vm(T, 3, Z + 4, 2, NX),
        vm(T, 3, 2, PIECE, NX),
        vm(T, 3, 2, PIECE, NX),
        vm(PIECES, 3, Z, PIECE, NX),
        vm(3, Z + 4, 8, NX),
        vm(Z + 2, 8, NX),
        vm(Z + 3, 8, NX),
        vm(Z + 3, 8, NX),
        vm(Z + 2, 8, NX),
        vm(3, Z, 8, NX),
        vm(Z + 2, 8, NX),
        dma(4), dma(2, 8), dma(2, total), dma(2, total), dma(2, STEPS * UPDATES),
        dma(2, T), dma(2, T), dma(2, T, 8), dma(2, T),
    ]
    anywhere = pl.BlockSpec(memory_space=pl.ANY)
    result = pl.pallas_call(
        functools.partial(kernel, T, K),
        out_shape=jax.ShapeDtypeStruct(starts.shape[1:], f32),
        in_specs=[anywhere] * 4 + [pl.BlockSpec(memory_space=pltpu.SMEM)],
        out_specs=pl.BlockSpec(memory_space=pltpu.VMEM),
        scratch_shapes=scratch,
        compiler_params=pltpu.CompilerParams(
            collective_id=0, has_side_effects=True, vmem_limit_bytes=48 * 1024 * 1024
        ),
    )(starts[0], source[0], mass_term, curve_entry, curve_table)
    return result[None]


def solution(mesh):
    return jax.shard_map(
        functools.partial(body, mesh),
        mesh=mesh,
        in_specs=(
            P("tm", None, "space", None, None),
            P("tm", None, "space", None, None),
            P("space", None, None),
            P("space", None, None),
            P(),
        ),
        out_specs=P("tm", None, "space", None, None),
        check_vma=False,
    )
```

```python
import functools

import jax
import jax.numpy as jnp
from jax import lax
from jax.experimental import pallas as pl
from jax.experimental.pallas import tpu as pltpu
from jax.sharding import PartitionSpec as P

STEPS = 2
UPDATES = 2
SWEEPS = 4
C_SWEEPS = 2
RELAX = 0.45

Z, NY, NX = 8, 32, 128
TBL = 64
PIECE = 4
PIECES = NY // PIECE
M = 2
N = M + 1
TOP = Z + M - 1
MID = Z // 2 - 1
LAST = MID
FINE = STEPS * UPDATES * SWEEPS


def next_y(v):
    return pltpu.roll(v, v.shape[-2] - 1, v.ndim - 2)


def next_x(v):
    return pltpu.roll(v, v.shape[-1] - 1, v.ndim - 1)


def prev_y(v):
    return pltpu.roll(v, 1, v.ndim - 2)


def prev_x(v):
    return pltpu.roll(v, 1, v.ndim - 1)


def curl_xy(v, above_x, above_y):
    x, y, z = v
    return (next_y(z) - z) - (above_y - y), (above_x - x) - (next_x(z) - z)


def curl_z(v):
    return (next_x(v[1]) - v[1]) - (next_y(v[0]) - v[0])


def curl(v, above_x, above_y):
    return (*curl_xy(v, above_x, above_y), curl_z(v))


def curl_adjoint(h, below_x, below_y):
    x, y, z = h
    return (
        (below_y - y) - (prev_y(z) - z),
        (prev_x(z) - z) - (below_x - x),
        (prev_y(x) - x) - (prev_x(y) - y),
    )


def reluctance(b, base, sat):
    squared = b[0] * b[0] + b[1] * b[1] + b[2] * b[2]
    return base * (1.0 + sat * squared / (1.0 + squared))


def step_sizes(mass, nu, below, relax):
    common = mass + 2.0 * nu
    before_y, before_x = prev_y(nu), prev_x(nu)
    return (
        relax / (common + below + before_y),
        relax / (common + below + before_x),
        relax / (common + before_y + before_x),
    )


def lag(z):
    return MID - z if z <= MID else z - MID - 1


def kernel(
    T, K,
    starts, source, mass, entry, table,
    out,
    X, X0, XC, SRC, S, E, BASE, SAT, NU, NUC, W, WC, R, PQ, V9, PQS, V9S,
    OLDV, OLDH,
    PS, CB, JS, JB, PB, SYU, SYD, YL, YH, ZL, ZH, OB, XW, MW, BW, SW, CW, RW,
    lsem, isem, psem, vsem, csem, jsem, hsem, osem,
):
    t = lax.axis_index("tm")
    k = lax.axis_index("space")
    up, down = lax.rem(k + 1, K), lax.rem(k + K - 1, K)

    def piece_of(d):
        odd = lax.rem(d, 2)
        half = d // 2
        return half * (1 - odd) + (T - 1 - half) * odd

    def group_of(i):
        low = jnp.where(i < T // 2, 1, 0)
        return 2 * i * low + (2 * T - 1 - 2 * i) * (1 - low)

    me = piece_of(t)
    right = group_of(lax.rem(me + 1, T))
    left = group_of(lax.rem(me + T - 1, T))

    def remote(src, dst, send, recv, tm, space):
        return pltpu.make_async_remote_copy(
            src_ref=src, dst_ref=dst, send_sem=send, recv_sem=recv,
            device_id=(tm, space), device_id_type=pl.DeviceIdType.MESH,
        )

    loads = [
        pltpu.make_async_copy(entry, E.at[N:N + Z], lsem.at[3]),
        pltpu.make_async_copy(starts, X0.at[:, N:N + Z], lsem.at[0]),
        pltpu.make_async_copy(source, SRC.at[:, M:M + Z], lsem.at[1]),
        pltpu.make_async_copy(mass, S.at[M:M + Z], lsem.at[2]),
    ]
    for load in loads:
        load.start()

    barrier = pltpu.get_barrier_semaphore()

    def greet(tm, space):
        pl.semaphore_signal(
            barrier, inc=1, device_id=(tm, space), device_id_type=pl.DeviceIdType.MESH
        )

    for space in (up, down):
        for tm in (t, left, right):
            greet(tm, space)
    for r in range(1, T):
        greet(lax.rem(t + r, T), k)

    keep_bottom = jnp.where(k > 0, 1.0, 0.0).astype(jnp.float32)
    keep_top = jnp.where(k < K - 1, 1.0, 0.0).astype(jnp.float32)

    def look_up(lo, hi):
        def plane(p, carry):
            cells = E[p]

            def one(j, acc):
                hit = cells == j
                return jnp.where(hit, table[0, j], acc[0]), jnp.where(hit, table[1, j], acc[1])

            zeros = jnp.zeros((NY, NX), jnp.float32)
            b, s = lax.fori_loop(0, TBL, one, (zeros, zeros))
            BASE[p] = b
            SAT[p] = s
            return carry

        lax.fori_loop(lo, hi, plane, 0)

    loads[0].wait()
    look_up(N, N + Z)

    pl.semaphore_wait(barrier, 6 + T - 1)

    first = [
        remote(entry.at[Z - N:Z], E.at[0:N], isem.at[0, 2], isem.at[1, 2], t, up),
        remote(entry.at[0:M], E.at[N + Z:N + Z + M], isem.at[0, 3], isem.at[1, 3], t, down),
        remote(starts.at[:, Z - N:Z], X0.at[:, 0:N], isem.at[0, 0], isem.at[1, 0], t, up),
        remote(starts.at[:, 0:N], X0.at[:, N + Z:], isem.at[0, 1], isem.at[1, 1], t, down),
        remote(mass.at[Z - M:Z], S.at[0:M], isem.at[0, 4], isem.at[1, 4], t, up),
        remote(mass.at[0:M], S.at[M + Z:], isem.at[0, 5], isem.at[1, 5], t, down),
        remote(source.at[:, Z - M:Z], SRC.at[:, 0:M], isem.at[0, 6], isem.at[1, 6], t, up),
        remote(source.at[:, 0:M], SRC.at[:, M + Z:], isem.at[0, 7], isem.at[1, 7], t, down),
    ]
    for copy in first:
        copy.start()

    for load in loads[1:]:
        load.wait()
    for c in range(3):
        X[c, N:N + Z] = X0[c, N:N + Z]

    def scatter(pieces, there, sem, verb):
        for r in range(1, T):
            d = lax.rem(t + r, T)
            copy = remote(pieces.at[piece_of(d)], there.at[t], sem.at[0, r], sem.at[1, t], d, k)
            getattr(copy, verb)()
        if verb == "start":
            pltpu.make_async_copy(pieces.at[me], there.at[t], sem.at[1, t]).start()

    def arrived(ref, sem):
        pltpu.make_async_copy(ref, ref, sem).wait()

    def window_of(v):
        return pltpu.roll(v, lax.rem(2 * NY + 2 - PIECE * me, NY), 0)[0:8]

    def chain_windows():
        for c in range(3):
            def window(p, carry, c=c):
                v = SRC[c, p + M - 1]
                even, odd = pltpu.roll(v, 2, 0), pltpu.roll(v, NY - 2, 0)
                for i in range(PIECES):
                    JS[i, c, p] = (odd if i % 2 else even)[8 * (i // 2):8 * (i // 2) + 8]
                return carry

            lax.fori_loop(0, Z + 2, window, 0)

        @pl.when(t < T - 1)
        def _():
            scatter(JS, JB, jsem, "start")

        for p in range(Z + 3):
            BW[p] = window_of(BASE[p + M - 1])
            SW[p] = window_of(SAT[p + M - 1])
        for p in range(Z + 2):
            MW[p] = window_of(S[p + M - 1]) * (1.0 / STEPS)
            RW[p] = jnp.full((8, NX), RELAX, jnp.float32) * (keep_top if p == Z + 1 else 1.0)

    def field(ref, z):
        return [ref[c, z + N] for c in range(3)]

    def low_parts(v):
        x, y, z = v
        return next_y(z) - z + y, next_x(z) - z + x, curl_z(v)

    def old_coarse():
        def above(ref, z):
            return ref[0, z + N + 1], ref[1, z + N + 1]

        def intensity(ref, z):
            b = curl(field(ref, z), *above(ref, z))
            return [NUC[z + N] * v for v in b]

        for z in range(-2, Z + 1):
            b = curl(field(X0, z), *above(X0, z))
            NUC[z + N] = reluctance(b, BASE[z + N], SAT[z + N])
        for z in range(-1, Z + 1):
            relax = RELAX * keep_top if z >= Z else RELAX
            w = step_sizes(S[z + M] * (1.0 / STEPS), NUC[z + N], NUC[z + N - 1], relax)
            for c in range(3):
                WC[c, z + M] = w[c]
        h = intensity(X0, -2)
        hx, hy = h[0], h[1]
        for z in range(-1, Z + 1):
            h = intensity(X0, z)
            a = curl_adjoint(h, hx, hy)
            for c in range(3):
                XC[c, z + N] = X0[c, z + N] + WC[c, z + M] * (SRC[c, z + M] - a[c])
            hx, hy = h[0], h[1]
        h = intensity(XC, -1)
        hx, hy = h[0], h[1]
        for z in range(Z):
            h = intensity(XC, z)
            a = curl_adjoint(h, hx, hy)
            for c in range(3):
                x = XC[c, z + N]
                drift = (1.0 / STEPS) * S[z + M] * (X0[c, z + N] - x)
                XC[c, z + N] = x + WC[c, z + M] * (SRC[c, z + M] + drift - a[c])
            hx, hy = h[0], h[1]

    def up_copy(slot):
        return remote(PQS.at[slot], PQ.at[slot], psem.at[0, slot], psem.at[1, slot], t, up)

    def down_copy(slot):
        return remote(V9S.at[slot], V9.at[slot], vsem.at[0, slot], vsem.at[1, slot], t, down)

    def engine(sweeps, total, rhs, begin, middle):
        def plane(a, i, z):
            level = sweeps * a + i - lag(z)
            n, place = (i - lag(z)) // sweeps + a, (i - lag(z)) % sweeps
            active = jnp.logical_and(level >= 0, level < total)
            slot = jnp.clip(level, 0, total - 1)
            is_first = place == 0
            x = field(X, z)
            mass_here = S[z + M]
            if z <= MID:
                if z == -M:
                    low = PQ[slot, 0] - x[1], x[0] - PQ[slot, 1], PQ[slot, 2]
                else:
                    under = field(X, z - 1)
                    low = curl_xy(under, x[0], x[1])
                    if is_first:
                        low = (*low, curl_z(under))
                if is_first:
                    NU[z + N - 1] = reluctance(low, BASE[z + N - 1], SAT[z + N - 1])
                nu_low = NU[z + N - 1]
                hx, hy = nu_low * low[0], nu_low * low[1]
                over = (X[0, z + N + 1], X[1, z + N + 1]) if z == MID else (OLDV[0, z + M + 1], OLDV[1, z + M + 1])
                b = curl(x, *over)
                if z == MID and is_first:
                    NU[z + N] = reluctance(b, BASE[z + N], SAT[z + N])
                if z > -M:
                    OLDV[0, z + M] = x[0]
                    OLDV[1, z + M] = x[1]
            else:
                over = (V9[slot, 0], V9[slot, 1]) if z == TOP else (X[0, z + N + 1], X[1, z + N + 1])
                b = curl(x, *over)
                if is_first:
                    NU[z + N] = reluctance(b, BASE[z + N], SAT[z + N])
                hx, hy = OLDH[0, z + M - 1], OLDH[1, z + M - 1]
            nu = NU[z + N]
            h = [nu * v for v in b]
            if MID <= z < TOP:
                OLDH[0, z + M] = h[0]
                OLDH[1, z + M] = h[1]
            if is_first:
                relax = RELAX * keep_top if z >= Z else RELAX
                w = step_sizes(mass_here, nu, NU[z + N - 1], relax)
                r = rhs(n, z, mass_here, x)
                for c in range(3):
                    W[c, z + M] = w[c]
                    R[c, z + M] = r[c]
            adj = curl_adjoint(h, hx, hy)
            new = []
            for c in range(3):
                v = x[c] + W[c, z + M] * (R[c, z + M] - mass_here * x[c] - adj[c])
                v = jnp.where(active, v, x[c])
                X[c, z + N] = v
                new.append(v)

        def step(a, i):
            s = sweeps * a + i

            @pl.when(s >= LAST + 1)
            def _():
                slot = s - (LAST + M)

                @pl.when(jnp.logical_and(slot >= 1, slot < total - M))
                def _():
                    up_copy(slot).wait_recv()
                    down_copy(slot).wait_recv()

                for z in range(-M, 0):
                    plane(a, i, z)
                for z in range(TOP, Z - 1, -1):
                    plane(a, i, z)

            for z in range(MID):
                plane(a, i, z)
            for z in range(Z - 1, MID + 1, -1):
                plane(a, i, z)
            plane(a, i, MID)
            plane(a, i, MID + 1)

            slot = s + 1 - lag(M)

            @pl.when(jnp.logical_and(slot >= 1, slot < total - M))
            def _():
                V9S[slot, 0] = X[0, M + N]
                V9S[slot, 1] = X[1, M + N]
                down_copy(slot).start()
                low = low_parts(field(X, Z - 1 - M))
                for c in range(3):
                    PQS[slot, c] = low[c]
                up_copy(slot).start()

        steps = total + LAST

        def block(a, carry):
            for i in range(sweeps):
                middle(a, i)
                if i == LAST % sweeps:
                    @pl.when(a == LAST // sweeps)
                    def _():
                        begin()

                if steps % sweeps and i >= steps % sweeps:
                    @pl.when(sweeps * a + i < steps)
                    def _():
                        step(a, i)
                else:
                    step(a, i)
            return carry

        lax.fori_loop(0, (steps + sweeps - 1) // sweeps, block, 0)

    def first_message(slot):
        V9[slot] = X[0:2, N + Z + M]
        low = low_parts(field(X, -N))
        for c in range(3):
            PQ[slot, c] = low[c]

    def begin_fine():
        first[0].wait_recv()
        first[1].wait_recv()
        look_up(0, N)
        look_up(N + Z, N + Z + M)
        BASE[0:N] = BASE[0:N] * keep_bottom
        for copy in first[2:]:
            copy.wait_recv()
        for c in range(3):
            X0[c, N + Z:] = X0[c, N + Z:] * keep_top
            X[c, 0:N] = X0[c, 0:N]
            X[c, N + Z:] = X0[c, N + Z:]
        first_message(0)

    def middle_fine(a, i):
        if i == 0:
            @pl.when(jnp.logical_and(a == 2, t < T - 1))
            def _():
                old_coarse()

            @pl.when(a == 1)
            def _():
                chain_windows()

    def rhs_fine(n, z, s, x):
        fresh = lax.rem(n + UPDATES, UPDATES) == 0
        return [jnp.where(fresh, s * x[c] + SRC[c, z + M], R[c, z + M]) for c in range(3)]

    engine(
        SWEEPS, FINE, rhs_fine, begin_fine, middle_fine
    )

    def pieces(z, carry):
        for c in range(3):
            v = jnp.where(t < T - 1, X[c, z + N] - XC[c, z + N], X[c, z + N])
            for i in range(PIECES):
                PS[i, c, z] = v[PIECE * i:PIECE * i + PIECE]
        return carry

    lax.fori_loop(0, Z, pieces, 0)
    scatter(PS, CB, csem, "start")

    arrived(CB.at[T - 1], csem.at[1, T - 1])
    for c in range(3):
        XW[c] = jnp.zeros((Z + 4, 8, NX), jnp.float32)
        CW[c] = jnp.zeros((Z, 8, NX), jnp.float32)
    for c in range(3):
        XW[c, 2:10, 2:6] = CB[T - 1, c]

    def out_remote(n):
        return remote(PB.at[n], OB.at[me], osem.at[0, n], osem.at[1, me], n, k)

    def emit(n):
        for c in range(3):
            PB[n, c] = XW[c, 2:10, 2:6]

        @pl.when(t != n)
        def _():
            out_remote(n).start()

        @pl.when(t == n)
        def _():
            pltpu.make_async_copy(PB.at[n], OB.at[me], osem.at[1, me]).start()

    def halos(n):
        s, r = hsem.at[0, n], hsem.at[1, n]
        return [
            remote(SYU.at[n], YL.at[n, :, 2:10], s.at[0], r.at[0], right, k),
            remote(SYD.at[n], YH.at[n, :, 2:10], s.at[1], r.at[1], left, k),
            remote(PB.at[n, :, 6:8], ZL.at[n], s.at[2], r.at[2], t, up),
            remote(PB.at[n, :, 0:2], ZH.at[n], s.at[3], r.at[3], t, down),
            remote(SYU.at[n, :, 6:8], YL.at[n, :, 0:2], s.at[4], r.at[4], right, up),
            remote(SYU.at[n, :, 0:2], YL.at[n, :, 10:12], s.at[5], r.at[5], right, down),
            remote(SYD.at[n, :, 6:8], YH.at[n, :, 0:2], s.at[6], r.at[6], left, up),
            remote(SYD.at[n, :, 0:2], YH.at[n, :, 10:12], s.at[7], r.at[7], left, down),
        ]

    def propagate(n, carry):
        for c in range(3):
            SYU[n, c] = XW[c, 2:10, 4:6]
            SYD[n, c] = XW[c, 2:10, 2:4]
        emit_first = halos(n)
        emit(n)
        for copy in emit_first:
            copy.start()
        arrived(JB.at[n], jsem.at[1, n])
        arrived(CB.at[n], csem.at[1, n])
        for c in range(3):
            CW[c, :, 2:6] = CB[n, c]
        for copy in emit_first:
            copy.wait_recv()
        for c in range(3):
            XW[c, :, 0:2] = YL[n, c]
            XW[c, :, 6:8] = YH[n, c]
            XW[c, 0:2, 2:6] = ZL[n, c]
            XW[c, 10:12, 2:6] = ZH[n, c]
            XW[c, 10:12] = XW[c, 10:12] * keep_top
        x0 = [XW[c] for c in range(3)]
        b = curl([v[:-1] for v in x0], x0[0][1:], x0[1][1:])
        nu = reluctance(b, BW[...], SW[...])
        h = [nu * v for v in b]
        w = step_sizes(MW[...], nu[1:], nu[:-1], RW[...])
        a = curl_adjoint([v[1:] for v in h], h[0][:-1], h[1][:-1])
        x1 = [x0[c][1:-1] + w[c] * (JB[n, c] - a[c]) for c in range(3)]
        b = curl([v[:-1] for v in x1], x1[0][1:], x1[1][1:])
        h = [nu[1:-1] * v for v in b]
        a = curl_adjoint([v[1:] for v in h], h[0][:-1], h[1][:-1])
        for c in range(3):
            x = x1[c][1:-1]
            drift = MW[1:9] * (x0[c][2:10] - x)
            x = x + w[c][1:-1] * (JB[n, c, 1:9] + drift - a[c])
            XW[c, 2:10] = x + CW[c]
        return carry

    lax.fori_loop(0, T - 1, propagate, 0)
    emit(T - 1)

    for i in range(PIECES):
        arrived(OB.at[i], osem.at[1, i])

    def place(z, carry):
        for c in range(3):
            for i in range(PIECES):
                XC[c, z, PIECE * i:PIECE * i + PIECE] = OB[i, c, z]
        return carry

    lax.fori_loop(0, Z, place, 0)
    store = pltpu.make_async_copy(XC.at[:, 0:Z], out, lsem.at[0])
    store.start()

    for copy in first:
        copy.wait_send()

    def sent(m, carry):
        up_copy(m).wait_send()
        down_copy(m).wait_send()
        return carry

    lax.fori_loop(1, FINE - M, sent, 0)
    scatter(PS, CB, csem, "wait_send")

    @pl.when(t < T - 1)
    def _():
        scatter(JS, JB, jsem, "wait_send")

    def halos_sent(n, carry):
        for copy in halos(n):
            copy.wait_send()
        return carry

    lax.fori_loop(0, T - 1, halos_sent, 0)

    def out_sent(n, carry):
        @pl.when(t != n)
        def _():
            out_remote(n).wait_send()

        return carry

    lax.fori_loop(0, T, out_sent, 0)
    store.wait()


def body(mesh, starts, source, mass_term, curve_entry, curve_table):
    T, K = mesh.shape["tm"], mesh.shape["space"]
    slots = FINE
    f32 = jnp.float32
    vm = lambda *shape: pltpu.VMEM((*shape, NY, NX), f32)
    rows = lambda *shape: pltpu.VMEM(shape, f32)
    dma = lambda *shape: pltpu.SemaphoreType.DMA(shape)
    scratch = [
        vm(3, Z + 2 * N),
        vm(3, Z + 2 * N),
        vm(3, Z + 2 * N),
        vm(3, Z + 2 * M),
        vm(Z + 2 * M),
        pltpu.VMEM((Z + 2 * M + 1, NY, NX), jnp.int32),
        vm(Z + 2 * M + 1),
        vm(Z + 2 * M + 1),
        vm(Z + 2 * M + 1),
        vm(Z + 2 * M + 1),
        vm(3, Z + 2 * M),
        vm(3, Z + 2 * M),
        vm(3, Z + 2 * M),
        vm(slots, 3),
        vm(slots, 2),
        vm(slots, 3),
        vm(slots, 2),
        vm(2, Z + 2 * M),
        vm(2, Z + 2 * M),
        rows(PIECES, 3, Z, PIECE, NX),
        rows(T, 3, Z, PIECE, NX),
        rows(PIECES, 3, Z + 2, 8, NX),
        rows(T, 3, Z + 2, 8, NX),
        rows(T, 3, Z, PIECE, NX),
        rows(T, 3, Z, 2, NX),
        rows(T, 3, Z, 2, NX),
        rows(T, 3, Z + 4, 2, NX),
        rows(T, 3, Z + 4, 2, NX),
        rows(T, 3, 2, PIECE, NX),
        rows(T, 3, 2, PIECE, NX),
        rows(PIECES, 3, Z, PIECE, NX),
        rows(3, Z + 4, 8, NX),
        rows(Z + 2, 8, NX),
        rows(Z + 3, 8, NX),
        rows(Z + 3, 8, NX),
        rows(3, Z, 8, NX),
        rows(Z + 2, 8, NX),
        dma(4), dma(2, 8), dma(2, FINE), dma(2, FINE),
        dma(2, T), dma(2, T), dma(2, T, 8), dma(2, T),
    ]
    anywhere = pl.BlockSpec(memory_space=pl.ANY)
    result = pl.pallas_call(
        functools.partial(kernel, T, K),
        out_shape=jax.ShapeDtypeStruct(starts.shape[1:], f32),
        in_specs=[anywhere] * 4 + [pl.BlockSpec(memory_space=pltpu.SMEM)],
        out_specs=anywhere,
        scratch_shapes=scratch,
        compiler_params=pltpu.CompilerParams(
            collective_id=0, has_side_effects=True, vmem_limit_bytes=60 * 1024 * 1024
        ),
    )(starts[0], source[0], mass_term, curve_entry, curve_table)
    return result[None]


def solution(mesh):
    return jax.shard_map(
        functools.partial(body, mesh),
        mesh=mesh,
        in_specs=(
            P("tm", None, "space", None, None),
            P("tm", None, "space", None, None),
            P("space", None, None),
            P("space", None, None),
            P(),
        ),
        out_specs=P("tm", None, "space", None, None),
        check_vma=False,
    )
```

```python
import functools

import jax
import jax.numpy as jnp
from jax import lax
from jax.experimental import pallas as pl
from jax.experimental.pallas import tpu as pltpu
from jax.sharding import PartitionSpec as P

STEPS = 2
UPDATES = 2
SWEEPS = 4
C_SWEEPS = 2
RELAX = 0.45

Z, NY, NX = 8, 32, 128
TBL = 64
PIECE = 4
PIECES = NY // PIECE
PACE = 1
M = 2
N = M + 1
TOP = Z + M - 1
MID = Z // 2 - 1
LAST = MID
FINE = STEPS * UPDATES * SWEEPS


def next_y(v):
    return pltpu.roll(v, v.shape[-2] - 1, v.ndim - 2)


def next_x(v):
    return pltpu.roll(v, v.shape[-1] - 1, v.ndim - 1)


def prev_y(v):
    return pltpu.roll(v, 1, v.ndim - 2)


def prev_x(v):
    return pltpu.roll(v, 1, v.ndim - 1)


def curl_xy(v, above_x, above_y):
    x, y, z = v
    return (next_y(z) - z) - (above_y - y), (above_x - x) - (next_x(z) - z)


def curl_z(v):
    return (next_x(v[1]) - v[1]) - (next_y(v[0]) - v[0])


def curl(v, above_x, above_y):
    return (*curl_xy(v, above_x, above_y), curl_z(v))


def curl_adjoint(h, below_x, below_y):
    x, y, z = h
    return (
        (below_y - y) - (prev_y(z) - z),
        (prev_x(z) - z) - (below_x - x),
        (prev_y(x) - x) - (prev_x(y) - y),
    )


def reluctance(b, base, sat):
    squared = b[0] * b[0] + b[1] * b[1] + b[2] * b[2]
    return base * (1.0 + sat * squared / (1.0 + squared))


def step_sizes(mass, nu, below, relax):
    common = mass + 2.0 * nu
    before_y, before_x = prev_y(nu), prev_x(nu)
    return (
        relax / (common + below + before_y),
        relax / (common + below + before_x),
        relax / (common + before_y + before_x),
    )


def lag(z):
    return MID - z if z <= MID else z - MID - 1


def kernel(
    T, K,
    starts, source, mass, entry, table,
    out,
    X, X0, XC, SRC, S, E, BASE, SAT, NU, NUC, W, WC, R, PQ, V9, PQS, V9S,
    OLDV, OLDH,
    PS, CB, JS, JB, PB, SYU, SYD, YL, YH, ZL, ZH, OB, XW, MW, BW, SW, CW, RW,
    lsem, isem, psem, vsem, csem, jsem, hsem, osem,
):
    t = lax.axis_index("tm")
    k = lax.axis_index("space")
    up, down = lax.rem(k + 1, K), lax.rem(k + K - 1, K)

    def piece_of(d):
        odd = lax.rem(d, 2)
        half = d // 2
        return half * (1 - odd) + (T - 1 - half) * odd

    def group_of(i):
        low = jnp.where(i < T // 2, 1, 0)
        return 2 * i * low + (2 * T - 1 - 2 * i) * (1 - low)

    me = piece_of(t)
    right = group_of(lax.rem(me + 1, T))
    left = group_of(lax.rem(me + T - 1, T))

    def remote(src, dst, send, recv, tm, space):
        return pltpu.make_async_remote_copy(
            src_ref=src, dst_ref=dst, send_sem=send, recv_sem=recv,
            device_id=(tm, space), device_id_type=pl.DeviceIdType.MESH,
        )

    loads = [
        pltpu.make_async_copy(entry, E, lsem.at[3]),
        pltpu.make_async_copy(starts, X0.at[:, N:N + Z], lsem.at[0]),
        pltpu.make_async_copy(source, SRC.at[:, M:M + Z], lsem.at[1]),
        pltpu.make_async_copy(mass, S.at[M:M + Z], lsem.at[2]),
    ]
    for load in loads:
        load.start()

    barrier = pltpu.get_barrier_semaphore()

    def greet(tm, space):
        pl.semaphore_signal(
            barrier, inc=1, device_id=(tm, space), device_id_type=pl.DeviceIdType.MESH
        )

    for space in (up, down):
        for tm in (t, left, right):
            greet(tm, space)
    for r in range(1, T):
        greet(lax.rem(t + r, T), k)

    keep_bottom = jnp.where(k > 0, 1.0, 0.0).astype(jnp.float32)
    keep_top = jnp.where(k < K - 1, 1.0, 0.0).astype(jnp.float32)

    def look_up(lo, hi):
        def plane(p, carry):
            cells = E[p - N]

            def one(j, acc):
                hit = cells == j
                return jnp.where(hit, table[0, j], acc[0]), jnp.where(hit, table[1, j], acc[1])

            zeros = jnp.zeros((NY, NX), jnp.float32)
            b, s = lax.fori_loop(0, TBL, one, (zeros, zeros))
            BASE[p] = b
            SAT[p] = s
            return carry

        lax.fori_loop(lo, hi, plane, 0)

    loads[0].wait()
    look_up(N, N + Z)

    pl.semaphore_wait(barrier, 6 + T - 1)

    first = [
        remote(BASE.at[Z:Z + N], BASE.at[0:N], isem.at[0, 2], isem.at[1, 2], t, up),
        remote(BASE.at[N:N + M], BASE.at[N + Z:], isem.at[0, 3], isem.at[1, 3], t, down),
        remote(SAT.at[Z:Z + N], SAT.at[0:N], isem.at[0, 8], isem.at[1, 8], t, up),
        remote(SAT.at[N:N + M], SAT.at[N + Z:], isem.at[0, 9], isem.at[1, 9], t, down),
        remote(starts.at[:, Z - N:Z], X0.at[:, 0:N], isem.at[0, 0], isem.at[1, 0], t, up),
        remote(starts.at[:, 0:N], X0.at[:, N + Z:], isem.at[0, 1], isem.at[1, 1], t, down),
        remote(mass.at[Z - M:Z], S.at[0:M], isem.at[0, 4], isem.at[1, 4], t, up),
        remote(mass.at[0:M], S.at[M + Z:], isem.at[0, 5], isem.at[1, 5], t, down),
        remote(source.at[:, Z - M:Z], SRC.at[:, 0:M], isem.at[0, 6], isem.at[1, 6], t, up),
        remote(source.at[:, 0:M], SRC.at[:, M + Z:], isem.at[0, 7], isem.at[1, 7], t, down),
    ]
    for copy in first:
        copy.start()

    for load in loads[1:]:
        load.wait()
    for c in range(3):
        X[c, N:N + Z] = X0[c, N:N + Z]

    def scatter(pieces, there, sem, verb):
        for r in range(1, T):
            d = lax.rem(t + r, T)
            copy = remote(pieces.at[piece_of(d)], there.at[t], sem.at[0, r], sem.at[1, t], d, k)
            getattr(copy, verb)()
        if verb == "start":
            pltpu.make_async_copy(pieces.at[me], there.at[t], sem.at[1, t]).start()

    def arrived(ref, sem):
        pltpu.make_async_copy(ref, ref, sem).wait()

    def window_of(v):
        return pltpu.roll(v, lax.rem(2 * NY + 2 - PIECE * me, NY), 0)[0:8]

    def chain_windows():
        for c in range(3):
            def window(p, carry, c=c):
                v = SRC[c, p + M - 1]
                even, odd = pltpu.roll(v, 2, 0), pltpu.roll(v, NY - 2, 0)
                for i in range(PIECES):
                    JS[i, c, p] = (odd if i % 2 else even)[8 * (i // 2):8 * (i // 2) + 8]
                return carry

            lax.fori_loop(0, Z + 2, window, 0)

        @pl.when(t < T - 1)
        def _():
            pltpu.make_async_copy(JS.at[me], JB.at[t], jsem.at[1, t]).start()

        for p in range(Z + 3):
            BW[p] = window_of(BASE[p + M - 1])
            SW[p] = window_of(SAT[p + M - 1])
        for p in range(Z + 2):
            MW[p] = window_of(S[p + M - 1]) * (1.0 / STEPS)
            RW[p] = jnp.full((8, NX), RELAX, jnp.float32) * (keep_top if p == Z + 1 else 1.0)

    def field(ref, z):
        return [ref[c, z + N] for c in range(3)]

    def low_parts(v):
        x, y, z = v
        return next_y(z) - z + y, next_x(z) - z + x, curl_z(v)

    def old_coarse():
        def above(ref, z):
            return ref[0, z + N + 1], ref[1, z + N + 1]

        def intensity(ref, z):
            b = curl(field(ref, z), *above(ref, z))
            return [NUC[z + N] * v for v in b]

        for z in range(-2, Z + 1):
            b = curl(field(X0, z), *above(X0, z))
            NUC[z + N] = reluctance(b, BASE[z + N], SAT[z + N])
        for z in range(-1, Z + 1):
            relax = RELAX * keep_top if z >= Z else RELAX
            w = step_sizes(S[z + M] * (1.0 / STEPS), NUC[z + N], NUC[z + N - 1], relax)
            for c in range(3):
                WC[c, z + M] = w[c]
        h = intensity(X0, -2)
        hx, hy = h[0], h[1]
        for z in range(-1, Z + 1):
            h = intensity(X0, z)
            a = curl_adjoint(h, hx, hy)
            for c in range(3):
                XC[c, z + N] = X0[c, z + N] + WC[c, z + M] * (SRC[c, z + M] - a[c])
            hx, hy = h[0], h[1]
        h = intensity(XC, -1)
        hx, hy = h[0], h[1]
        for z in range(Z):
            h = intensity(XC, z)
            a = curl_adjoint(h, hx, hy)
            for c in range(3):
                x = XC[c, z + N]
                drift = (1.0 / STEPS) * S[z + M] * (X0[c, z + N] - x)
                XC[c, z + N] = x + WC[c, z + M] * (SRC[c, z + M] + drift - a[c])
            hx, hy = h[0], h[1]

    def up_copy(slot):
        return remote(PQS.at[slot], PQ.at[slot], psem.at[0, slot], psem.at[1, slot], t, up)

    def down_copy(slot):
        return remote(V9S.at[slot], V9.at[slot], vsem.at[0, slot], vsem.at[1, slot], t, down)

    def engine(sweeps, total, rhs, begin, middle):
        def plane(a, i, z):
            level = sweeps * a + i - lag(z)
            n, place = (i - lag(z)) // sweeps + a, (i - lag(z)) % sweeps
            active = jnp.logical_and(level >= 0, level < total)
            slot = jnp.clip(level, 0, total - 1)
            is_first = place == 0
            x = field(X, z)
            mass_here = S[z + M]
            if z <= MID:
                if z == -M:
                    low = PQ[slot, 0] - x[1], x[0] - PQ[slot, 1], PQ[slot, 2]
                else:
                    under = field(X, z - 1)
                    low = curl_xy(under, x[0], x[1])
                    if is_first:
                        low = (*low, curl_z(under))
                if is_first:
                    NU[z + N - 1] = reluctance(low, BASE[z + N - 1], SAT[z + N - 1])
                nu_low = NU[z + N - 1]
                hx, hy = nu_low * low[0], nu_low * low[1]
                over = (X[0, z + N + 1], X[1, z + N + 1]) if z == MID else (OLDV[0, z + M + 1], OLDV[1, z + M + 1])
                b = curl(x, *over)
                if z == MID and is_first:
                    NU[z + N] = reluctance(b, BASE[z + N], SAT[z + N])
                if z > -M:
                    OLDV[0, z + M] = x[0]
                    OLDV[1, z + M] = x[1]
            else:
                over = (V9[slot, 0], V9[slot, 1]) if z == TOP else (X[0, z + N + 1], X[1, z + N + 1])
                b = curl(x, *over)
                if is_first:
                    NU[z + N] = reluctance(b, BASE[z + N], SAT[z + N])
                hx, hy = OLDH[0, z + M - 1], OLDH[1, z + M - 1]
            nu = NU[z + N]
            h = [nu * v for v in b]
            if MID <= z < TOP:
                OLDH[0, z + M] = h[0]
                OLDH[1, z + M] = h[1]
            if is_first:
                relax = RELAX * keep_top if z >= Z else RELAX
                w = step_sizes(mass_here, nu, NU[z + N - 1], relax)
                r = rhs(n, z, mass_here, x)
                for c in range(3):
                    W[c, z + M] = w[c]
                    R[c, z + M] = r[c]
            adj = curl_adjoint(h, hx, hy)
            new = []
            for c in range(3):
                v = x[c] + W[c, z + M] * (R[c, z + M] - mass_here * x[c] - adj[c])
                v = jnp.where(active, v, x[c])
                X[c, z + N] = v
                new.append(v)

        def step(a, i):
            s = sweeps * a + i

            @pl.when(s >= LAST + 1)
            def _():
                slot = s - (LAST + M)

                @pl.when(jnp.logical_and(slot >= 1, slot < total - M))
                def _():
                    up_copy(slot).wait_recv()
                    down_copy(slot).wait_recv()

                for z in range(-M, 0):
                    plane(a, i, z)
                for z in range(TOP, Z - 1, -1):
                    plane(a, i, z)

            for z in range(MID):
                plane(a, i, z)
            for z in range(Z - 1, MID + 1, -1):
                plane(a, i, z)
            plane(a, i, MID)
            plane(a, i, MID + 1)

            slot = s + 1 - lag(M)

            @pl.when(jnp.logical_and(slot >= 1, slot < total - M))
            def _():
                V9S[slot, 0] = X[0, M + N]
                V9S[slot, 1] = X[1, M + N]
                down_copy(slot).start()
                low = low_parts(field(X, Z - 1 - M))
                for c in range(3):
                    PQS[slot, c] = low[c]
                up_copy(slot).start()

        steps = total + LAST

        def block(a, carry):
            for i in range(sweeps):
                middle(a, i)
                if i == LAST % sweeps:
                    @pl.when(a == LAST // sweeps)
                    def _():
                        begin()

                if steps % sweeps and i >= steps % sweeps:
                    @pl.when(sweeps * a + i < steps)
                    def _():
                        step(a, i)
                else:
                    step(a, i)
            return carry

        lax.fori_loop(0, (steps + sweeps - 1) // sweeps, block, 0)

    def first_message(slot):
        V9[slot] = X[0:2, N + Z + M]
        low = low_parts(field(X, -N))
        for c in range(3):
            PQ[slot, c] = low[c]

    def begin_fine():
        for copy in first:
            copy.wait_recv()
        BASE[0:N] = BASE[0:N] * keep_bottom
        for c in range(3):
            X0[c, N + Z:] = X0[c, N + Z:] * keep_top
            X[c, 0:N] = X0[c, 0:N]
            X[c, N + Z:] = X0[c, N + Z:]
        first_message(0)

    def middle_fine(a, i):
        if i == 0:
            @pl.when(jnp.logical_and(a == 2, t < T - 1))
            def _():
                old_coarse()

            @pl.when(a == 1)
            def _():
                chain_windows()

        r = (SWEEPS * a + i - SWEEPS) // PACE + 1

        @pl.when(jnp.logical_and((SWEEPS * a + i) % PACE == 0, jnp.logical_and(t < T - 1, jnp.logical_and(a >= 1, r < T))))
        def _():
            d = lax.rem(t + r, T)
            remote(JS.at[piece_of(d)], JB.at[t], jsem.at[0, r], jsem.at[1, t], d, k).start()

    def rhs_fine(n, z, s, x):
        fresh = lax.rem(n + UPDATES, UPDATES) == 0
        return [jnp.where(fresh, s * x[c] + SRC[c, z + M], R[c, z + M]) for c in range(3)]

    engine(
        SWEEPS, FINE, rhs_fine, begin_fine, middle_fine
    )

    def pieces(z, carry):
        for c in range(3):
            v = jnp.where(t < T - 1, X[c, z + N] - XC[c, z + N], X[c, z + N])
            for i in range(PIECES):
                PS[i, c, z] = v[PIECE * i:PIECE * i + PIECE]
        return carry

    lax.fori_loop(0, Z, pieces, 0)
    scatter(PS, CB, csem, "start")

    arrived(CB.at[T - 1], csem.at[1, T - 1])
    for c in range(3):
        XW[c] = jnp.zeros((Z + 4, 8, NX), jnp.float32)
        CW[c] = jnp.zeros((Z, 8, NX), jnp.float32)
    for c in range(3):
        XW[c, 2:10, 2:6] = CB[T - 1, c]

    def out_remote(n):
        return remote(PB.at[n], OB.at[me], osem.at[0, n], osem.at[1, me], n, k)

    def emit(n):
        @pl.when(t != n)
        def _():
            out_remote(n).start()

        @pl.when(t == n)
        def _():
            pltpu.make_async_copy(PB.at[n], OB.at[me], osem.at[1, me]).start()

    def halos(n):
        s, r = hsem.at[0, n], hsem.at[1, n]
        return [
            remote(SYU.at[n], YL.at[n, :, 2:10], s.at[0], r.at[0], right, k),
            remote(SYD.at[n], YH.at[n, :, 2:10], s.at[1], r.at[1], left, k),
            remote(PB.at[n, :, 6:8], ZL.at[n], s.at[2], r.at[2], t, up),
            remote(PB.at[n, :, 0:2], ZH.at[n], s.at[3], r.at[3], t, down),
            remote(SYU.at[n, :, 6:8], YL.at[n, :, 0:2], s.at[4], r.at[4], right, up),
            remote(SYU.at[n, :, 0:2], YL.at[n, :, 10:12], s.at[5], r.at[5], right, down),
            remote(SYD.at[n, :, 6:8], YH.at[n, :, 0:2], s.at[6], r.at[6], left, up),
            remote(SYD.at[n, :, 0:2], YH.at[n, :, 10:12], s.at[7], r.at[7], left, down),
        ]

    def propagate(n, carry):
        for c in range(3):
            SYU[n, c] = XW[c, 2:10, 4:6]
            SYD[n, c] = XW[c, 2:10, 2:4]
        emit_first = halos(n)
        for copy in emit_first[4:] + emit_first[:2]:
            copy.start()
        for c in range(3):
            PB[n, c] = XW[c, 2:10, 2:6]
        for copy in emit_first[2:4]:
            copy.start()
        emit(n)
        arrived(JB.at[n], jsem.at[1, n])
        arrived(CB.at[n], csem.at[1, n])
        for c in range(3):
            CW[c, :, 2:6] = CB[n, c]
        for copy in emit_first:
            copy.wait_recv()
        for c in range(3):
            XW[c, :, 0:2] = YL[n, c]
            XW[c, :, 6:8] = YH[n, c]
            XW[c, 0:2, 2:6] = ZL[n, c]
            XW[c, 10:12, 2:6] = ZH[n, c]
            XW[c, 10:12] = XW[c, 10:12] * keep_top
        x0 = [XW[c] for c in range(3)]
        b = curl([v[:-1] for v in x0], x0[0][1:], x0[1][1:])
        nu = reluctance(b, BW[...], SW[...])
        h = [nu * v for v in b]
        w = step_sizes(MW[...], nu[1:], nu[:-1], RW[...])
        a = curl_adjoint([v[1:] for v in h], h[0][:-1], h[1][:-1])
        x1 = [x0[c][1:-1] + w[c] * (JB[n, c] - a[c]) for c in range(3)]
        b = curl([v[:-1] for v in x1], x1[0][1:], x1[1][1:])
        h = [nu[1:-1] * v for v in b]
        a = curl_adjoint([v[1:] for v in h], h[0][:-1], h[1][:-1])
        for c in range(3):
            x = x1[c][1:-1]
            drift = MW[1:9] * (x0[c][2:10] - x)
            x = x + w[c][1:-1] * (JB[n, c, 1:9] + drift - a[c])
            XW[c, 2:10] = x + CW[c]
        return carry

    lax.fori_loop(0, T - 1, propagate, 0)
    for c in range(3):
        PB[T - 1, c] = XW[c, 2:10, 2:6]
    emit(T - 1)

    for i in range(PIECES):
        arrived(OB.at[i], osem.at[1, i])

    def place(z, carry):
        for c in range(3):
            for i in range(PIECES):
                XC[c, z, PIECE * i:PIECE * i + PIECE] = OB[i, c, z]
        return carry

    lax.fori_loop(0, Z, place, 0)
    store = pltpu.make_async_copy(XC.at[:, 0:Z], out, lsem.at[0])
    store.start()

    for copy in first:
        copy.wait_send()

    def sent(m, carry):
        up_copy(m).wait_send()
        down_copy(m).wait_send()
        return carry

    lax.fori_loop(1, FINE - M, sent, 0)
    scatter(PS, CB, csem, "wait_send")

    @pl.when(t < T - 1)
    def _():
        scatter(JS, JB, jsem, "wait_send")

    def halos_sent(n, carry):
        for copy in halos(n):
            copy.wait_send()
        return carry

    lax.fori_loop(0, T - 1, halos_sent, 0)

    def out_sent(n, carry):
        @pl.when(t != n)
        def _():
            out_remote(n).wait_send()

        return carry

    lax.fori_loop(0, T, out_sent, 0)
    store.wait()


def body(mesh, starts, source, mass_term, curve_entry, curve_table):
    T, K = mesh.shape["tm"], mesh.shape["space"]
    slots = FINE
    f32 = jnp.float32
    vm = lambda *shape: pltpu.VMEM((*shape, NY, NX), f32)
    rows = lambda *shape: pltpu.VMEM(shape, f32)
    dma = lambda *shape: pltpu.SemaphoreType.DMA(shape)
    scratch = [
        vm(3, Z + 2 * N),
        vm(3, Z + 2 * N),
        vm(3, Z + 2 * N),
        vm(3, Z + 2 * M),
        vm(Z + 2 * M),
        pltpu.VMEM((Z, NY, NX), jnp.int32),
        vm(Z + 2 * M + 1),
        vm(Z + 2 * M + 1),
        vm(Z + 2 * M + 1),
        vm(Z + 2 * M + 1),
        vm(3, Z + 2 * M),
        vm(3, Z + 2 * M),
        vm(3, Z + 2 * M),
        vm(slots, 3),
        vm(slots, 2),
        vm(slots, 3),
        vm(slots, 2),
        vm(2, Z + 2 * M),
        vm(2, Z + 2 * M),
        rows(PIECES, 3, Z, PIECE, NX),
        rows(T, 3, Z, PIECE, NX),
        rows(PIECES, 3, Z + 2, 8, NX),
        rows(T, 3, Z + 2, 8, NX),
        rows(T, 3, Z, PIECE, NX),
        rows(T, 3, Z, 2, NX),
        rows(T, 3, Z, 2, NX),
        rows(T, 3, Z + 4, 2, NX),
        rows(T, 3, Z + 4, 2, NX),
        rows(T, 3, 2, PIECE, NX),
        rows(T, 3, 2, PIECE, NX),
        rows(PIECES, 3, Z, PIECE, NX),
        rows(3, Z + 4, 8, NX),
        rows(Z + 2, 8, NX),
        rows(Z + 3, 8, NX),
        rows(Z + 3, 8, NX),
        rows(3, Z, 8, NX),
        rows(Z + 2, 8, NX),
        dma(4), dma(2, 10), dma(2, FINE), dma(2, FINE),
        dma(2, T), dma(2, T), dma(2, T, 8), dma(2, T),
    ]
    anywhere = pl.BlockSpec(memory_space=pl.ANY)
    result = pl.pallas_call(
        functools.partial(kernel, T, K),
        out_shape=jax.ShapeDtypeStruct(starts.shape[1:], f32),
        in_specs=[anywhere] * 4 + [pl.BlockSpec(memory_space=pltpu.SMEM)],
        out_specs=anywhere,
        scratch_shapes=scratch,
        compiler_params=pltpu.CompilerParams(
            collective_id=0, has_side_effects=True, vmem_limit_bytes=60 * 1024 * 1024
        ),
    )(starts[0], source[0], mass_term, curve_entry, curve_table)
    return result[None]


def solution(mesh):
    return jax.shard_map(
        functools.partial(body, mesh),
        mesh=mesh,
        in_specs=(
            P("tm", None, "space", None, None),
            P("tm", None, "space", None, None),
            P("space", None, None),
            P("space", None, None),
            P(),
        ),
        out_specs=P("tm", None, "space", None, None),
        check_vma=False,
    )
```

```python
import functools

import jax
import jax.numpy as jnp
from jax import lax
from jax.experimental import pallas as pl
from jax.experimental.pallas import tpu as pltpu
from jax.sharding import PartitionSpec as P

STEPS = 2
UPDATES = 2
SWEEPS = 4
C_SWEEPS = 2
RELAX = 0.45

Z, NY, NX = 8, 32, 128
TBL = 64
PIECE = 4
PIECES = NY // PIECE
PACE = 1
M = 2
N = M + 1
TOP = Z + M - 1
MID = Z // 2 - 1
LAST = MID
FINE = STEPS * UPDATES * SWEEPS


def next_y(v):
    return pltpu.roll(v, v.shape[-2] - 1, v.ndim - 2)


def next_x(v):
    return pltpu.roll(v, v.shape[-1] - 1, v.ndim - 1)


def prev_y(v):
    return pltpu.roll(v, 1, v.ndim - 2)


def prev_x(v):
    return pltpu.roll(v, 1, v.ndim - 1)


def curl_xy(v, above_x, above_y):
    x, y, z = v
    return (next_y(z) - z) - (above_y - y), (above_x - x) - (next_x(z) - z)


def curl_z(v):
    return (next_x(v[1]) - v[1]) - (next_y(v[0]) - v[0])


def curl(v, above_x, above_y):
    return (*curl_xy(v, above_x, above_y), curl_z(v))


def curl_adjoint(h, below_x, below_y):
    x, y, z = h
    return (
        (below_y - y) - (prev_y(z) - z),
        (prev_x(z) - z) - (below_x - x),
        (prev_y(x) - x) - (prev_x(y) - y),
    )


def reluctance(b, base, sat):
    squared = b[0] * b[0] + b[1] * b[1] + b[2] * b[2]
    return base * (1.0 + sat * squared / (1.0 + squared))


def step_sizes(mass, nu, below, relax):
    common = mass + 2.0 * nu
    before_y, before_x = prev_y(nu), prev_x(nu)
    return (
        relax / (common + below + before_y),
        relax / (common + below + before_x),
        relax / (common + before_y + before_x),
    )


def lag(z):
    return MID - z if z <= MID else z - MID - 1


def kernel(
    T, K,
    starts, source, mass, entry, table,
    out,
    X, X0, XC, SRC, S, E, BASE, SAT, NU, NUC, W, WC, R, PQ, V9, HZ, PQS, V9S,
    OLDV, OLDH,
    PS, CB, JS, JT, JB, JC, JW, PB, SYU, SYD, YL, YH, ZL, ZH, OB, XW, MW, BW, SW, CW, RW,
    lsem, isem, psem, vsem, zsem, csem, jsem, ksem, hsem, osem,
):
    t = lax.axis_index("tm")
    k = lax.axis_index("space")
    up, down = lax.rem(k + 1, K), lax.rem(k + K - 1, K)

    def piece_of(d):
        odd = lax.rem(d, 2)
        half = d // 2
        return half * (1 - odd) + (T - 1 - half) * odd

    def group_of(i):
        low = jnp.where(i < T // 2, 1, 0)
        return 2 * i * low + (2 * T - 1 - 2 * i) * (1 - low)

    me = piece_of(t)
    right = group_of(lax.rem(me + 1, T))
    left = group_of(lax.rem(me + T - 1, T))

    def remote(src, dst, send, recv, tm, space):
        return pltpu.make_async_remote_copy(
            src_ref=src, dst_ref=dst, send_sem=send, recv_sem=recv,
            device_id=(tm, space), device_id_type=pl.DeviceIdType.MESH,
        )

    loads = [
        pltpu.make_async_copy(entry, E, lsem.at[3]),
        pltpu.make_async_copy(starts, X0.at[:, N:N + Z], lsem.at[0]),
        pltpu.make_async_copy(source, SRC.at[:, M:M + Z], lsem.at[1]),
        pltpu.make_async_copy(mass, S.at[M:M + Z], lsem.at[2]),
    ]
    for load in loads:
        load.start()

    barrier = pltpu.get_barrier_semaphore()

    def greet(tm, space):
        pl.semaphore_signal(
            barrier, inc=1, device_id=(tm, space), device_id_type=pl.DeviceIdType.MESH
        )

    for space in (up, down):
        for tm in (t, left, right):
            greet(tm, space)
    for r in range(1, T):
        greet(lax.rem(t + r, T), k)

    keep_bottom = jnp.where(k > 0, 1.0, 0.0).astype(jnp.float32)
    keep_top = jnp.where(k < K - 1, 1.0, 0.0).astype(jnp.float32)

    def look_up(lo, hi):
        def plane(p, carry):
            cells = E[p - N]

            def one(j, acc):
                hit = cells == j
                return jnp.where(hit, table[0, j], acc[0]), jnp.where(hit, table[1, j], acc[1])

            zeros = jnp.zeros((NY, NX), jnp.float32)
            b, s = lax.fori_loop(0, TBL, one, (zeros, zeros))
            BASE[p] = b
            SAT[p] = s
            return carry

        lax.fori_loop(lo, hi, plane, 0)

    loads[0].wait()
    look_up(N, N + Z)

    pl.semaphore_wait(barrier, 6 + T - 1)

    first = [
        remote(BASE.at[Z:Z + N], BASE.at[0:N], isem.at[0, 2], isem.at[1, 2], t, up),
        remote(BASE.at[N:N + M], BASE.at[N + Z:], isem.at[0, 3], isem.at[1, 3], t, down),
        remote(SAT.at[Z:Z + N], SAT.at[0:N], isem.at[0, 8], isem.at[1, 8], t, up),
        remote(SAT.at[N:N + M], SAT.at[N + Z:], isem.at[0, 9], isem.at[1, 9], t, down),
        remote(starts.at[:, Z - N:Z], X0.at[:, 0:N], isem.at[0, 0], isem.at[1, 0], t, up),
        remote(starts.at[:, 0:N], X0.at[:, N + Z:], isem.at[0, 1], isem.at[1, 1], t, down),
        remote(mass.at[Z - M:Z], S.at[0:M], isem.at[0, 4], isem.at[1, 4], t, up),
        remote(mass.at[0:M], S.at[M + Z:], isem.at[0, 5], isem.at[1, 5], t, down),
        remote(source.at[:, Z - M:Z], SRC.at[:, 0:M], isem.at[0, 6], isem.at[1, 6], t, up),
        remote(source.at[:, 0:M], SRC.at[:, M + Z:], isem.at[0, 7], isem.at[1, 7], t, down),
    ]
    for copy in first:
        copy.start()

    for load in loads[1:]:
        load.wait()
    for c in range(3):
        X[c, N:N + Z] = X0[c, N:N + Z]

    def scatter(pieces, there, sem, verb):
        for r in range(1, T):
            d = lax.rem(t + r, T)
            copy = remote(pieces.at[piece_of(d)], there.at[t], sem.at[0, r], sem.at[1, t], d, k)
            getattr(copy, verb)()
        if verb == "start":
            pltpu.make_async_copy(pieces.at[me], there.at[t], sem.at[1, t]).start()

    def arrived(ref, sem):
        pltpu.make_async_copy(ref, ref, sem).wait()

    def window_of(v):
        return pltpu.roll(v, lax.rem(2 * NY + 2 - PIECE * me, NY), 0)[0:8]

    def chain_windows():
        for c in range(3):
            def window(p, carry, c=c):
                v = SRC[c, p + M - 1]
                even, odd = pltpu.roll(v, 1, 0), pltpu.roll(v, NY - 3, 0)
                for i in range(PIECES):
                    rows = (odd if i % 2 else even)[8 * (i // 2):8 * (i // 2) + 8]
                    JS[i, c, p] = rows[0:4]
                    JT[i, c, p] = rows[4:6]
                return carry

            lax.fori_loop(0, Z + 2, window, 0)

        @pl.when(t < T - 1)
        def _():
            pltpu.make_async_copy(JS.at[me], JB.at[t], jsem.at[1, t]).start()
            pltpu.make_async_copy(JT.at[me], JC.at[t], ksem.at[1, t]).start()

        for p in range(Z + 3):
            BW[p] = window_of(BASE[p + M - 1])
            SW[p] = window_of(SAT[p + M - 1])
        for p in range(Z + 2):
            MW[p] = window_of(S[p + M - 1]) * (1.0 / STEPS)
            RW[p] = jnp.full((8, NX), RELAX, jnp.float32) * (keep_top if p == Z + 1 else 1.0)

    def field(ref, z):
        return [ref[c, z + N] for c in range(3)]

    def low_parts(v):
        x, y, z = v
        return next_y(z) - z + y, next_x(z) - z + x, curl_z(v)

    def old_coarse():
        def above(ref, z):
            return ref[0, z + N + 1], ref[1, z + N + 1]

        def intensity(ref, z):
            b = curl(field(ref, z), *above(ref, z))
            return [NUC[z + N] * v for v in b]

        for z in range(-2, Z + 1):
            b = curl(field(X0, z), *above(X0, z))
            NUC[z + N] = reluctance(b, BASE[z + N], SAT[z + N])
        for z in range(-1, Z + 1):
            relax = RELAX * keep_top if z >= Z else RELAX
            w = step_sizes(S[z + M] * (1.0 / STEPS), NUC[z + N], NUC[z + N - 1], relax)
            for c in range(3):
                WC[c, z + M] = w[c]
        h = intensity(X0, -2)
        hx, hy = h[0], h[1]
        for z in range(-1, Z + 1):
            h = intensity(X0, z)
            a = curl_adjoint(h, hx, hy)
            for c in range(3):
                XC[c, z + N] = X0[c, z + N] + WC[c, z + M] * (SRC[c, z + M] - a[c])
            hx, hy = h[0], h[1]
        h = intensity(XC, -1)
        hx, hy = h[0], h[1]
        for z in range(Z):
            h = intensity(XC, z)
            a = curl_adjoint(h, hx, hy)
            for c in range(3):
                x = XC[c, z + N]
                drift = (1.0 / STEPS) * S[z + M] * (X0[c, z + N] - x)
                XC[c, z + N] = x + WC[c, z + M] * (SRC[c, z + M] + drift - a[c])
            hx, hy = h[0], h[1]

    def up_copy(slot):
        return remote(PQS.at[slot], PQ.at[slot], psem.at[0, slot], psem.at[1, slot], t, up)

    def hz_copy(u):
        return remote(HZ.at[0, u], HZ.at[1, u], zsem.at[0, u], zsem.at[1, u], t, up)

    def down_copy(slot):
        return remote(V9S.at[slot], V9.at[slot], vsem.at[0, slot], vsem.at[1, slot], t, down)

    def engine(sweeps, total, rhs, begin, middle):
        def plane(a, i, z):
            level = sweeps * a + i - lag(z)
            n, place = (i - lag(z)) // sweeps + a, (i - lag(z)) % sweeps
            active = jnp.logical_and(level >= 0, level < total)
            slot = jnp.clip(level, 0, total - 1)
            is_first = place == 0
            x = field(X, z)
            mass_here = S[z + M]
            if z <= MID:
                if z == -M:
                    low = PQ[slot, 0] - x[1], x[0] - PQ[slot, 1]
                    if is_first:
                        low = (*low, HZ[1, jnp.clip(n, 0, total // sweeps - 1)])
                else:
                    under = field(X, z - 1)
                    low = curl_xy(under, x[0], x[1])
                    if is_first:
                        low = (*low, curl_z(under))
                if is_first:
                    NU[z + N - 1] = reluctance(low, BASE[z + N - 1], SAT[z + N - 1])
                nu_low = NU[z + N - 1]
                hx, hy = nu_low * low[0], nu_low * low[1]
                over = (X[0, z + N + 1], X[1, z + N + 1]) if z == MID else (OLDV[0, z + M + 1], OLDV[1, z + M + 1])
                b = curl(x, *over)
                if z == MID and is_first:
                    NU[z + N] = reluctance(b, BASE[z + N], SAT[z + N])
                if z > -M:
                    OLDV[0, z + M] = x[0]
                    OLDV[1, z + M] = x[1]
            else:
                over = (V9[slot, 0], V9[slot, 1]) if z == TOP else (X[0, z + N + 1], X[1, z + N + 1])
                b = curl(x, *over)
                if is_first:
                    NU[z + N] = reluctance(b, BASE[z + N], SAT[z + N])
                hx, hy = OLDH[0, z + M - 1], OLDH[1, z + M - 1]
            nu = NU[z + N]
            h = [nu * v for v in b]
            if MID <= z < TOP:
                OLDH[0, z + M] = h[0]
                OLDH[1, z + M] = h[1]
            if is_first:
                relax = RELAX * keep_top if z >= Z else RELAX
                w = step_sizes(mass_here, nu, NU[z + N - 1], relax)
                r = rhs(n, z, mass_here, x)
                for c in range(3):
                    W[c, z + M] = w[c]
                    R[c, z + M] = r[c]
            adj = curl_adjoint(h, hx, hy)
            new = []
            for c in range(3):
                v = x[c] + W[c, z + M] * (R[c, z + M] - mass_here * x[c] - adj[c])
                v = jnp.where(active, v, x[c])
                X[c, z + N] = v
                new.append(v)

        def step(a, i):
            s = sweeps * a + i

            @pl.when(s >= LAST + 1)
            def _():
                slot = s - (LAST + M)

                @pl.when(jnp.logical_and(slot >= 1, slot < total - M))
                def _():
                    up_copy(slot).wait_recv()
                    down_copy(slot).wait_recv()
                    if (i - LAST - M) % sweeps == 0:
                        hz_copy(a + (i - LAST - M) // sweeps).wait_recv()

                for z in range(-M, 0):
                    plane(a, i, z)
                for z in range(TOP, Z - 1, -1):
                    plane(a, i, z)

            for z in range(MID):
                plane(a, i, z)
            for z in range(Z - 1, MID + 1, -1):
                plane(a, i, z)
            plane(a, i, MID)
            plane(a, i, MID + 1)

            slot = s + 1 - lag(M)

            @pl.when(jnp.logical_and(slot >= 1, slot < total - M))
            def _():
                V9S[slot, 0] = X[0, M + N]
                V9S[slot, 1] = X[1, M + N]
                down_copy(slot).start()
                low = low_parts(field(X, Z - 1 - M))
                PQS[slot, 0] = low[0]
                PQS[slot, 1] = low[1]
                up_copy(slot).start()
                if (i + 1 - lag(M)) % sweeps == 0:
                    u = a + (i + 1 - lag(M)) // sweeps
                    HZ[0, u] = low[2]
                    hz_copy(u).start()

        steps = total + LAST

        def block(a, carry):
            for i in range(sweeps):
                middle(a, i)
                if i == LAST % sweeps:
                    @pl.when(a == LAST // sweeps)
                    def _():
                        begin()

                if steps % sweeps and i >= steps % sweeps:
                    @pl.when(sweeps * a + i < steps)
                    def _():
                        step(a, i)
                else:
                    step(a, i)
            return carry

        lax.fori_loop(0, (steps + sweeps - 1) // sweeps, block, 0)

    def first_message(slot):
        V9[slot] = X[0:2, N + Z + M]
        low = low_parts(field(X, -N))
        PQ[slot, 0] = low[0]
        PQ[slot, 1] = low[1]
        HZ[1, slot] = low[2]

    def begin_fine():
        for copy in first:
            copy.wait_recv()
        BASE[0:N] = BASE[0:N] * keep_bottom
        for c in range(3):
            X0[c, N + Z:] = X0[c, N + Z:] * keep_top
            X[c, 0:N] = X0[c, 0:N]
            X[c, N + Z:] = X0[c, N + Z:]
        first_message(0)

    def middle_fine(a, i):
        if i == 0:
            @pl.when(jnp.logical_and(a == 2, t < T - 1))
            def _():
                old_coarse()

            @pl.when(a == 1)
            def _():
                chain_windows()

        r = (SWEEPS * a + i - SWEEPS) // PACE + 1

        @pl.when(jnp.logical_and((SWEEPS * a + i) % PACE == 0, jnp.logical_and(t < T - 1, jnp.logical_and(a >= 1, r < T))))
        def _():
            d = lax.rem(t + r, T)
            remote(JS.at[piece_of(d)], JB.at[t], jsem.at[0, r], jsem.at[1, t], d, k).start()
            remote(JT.at[piece_of(d)], JC.at[t], ksem.at[0, r], ksem.at[1, t], d, k).start()

    def rhs_fine(n, z, s, x):
        fresh = lax.rem(n + UPDATES, UPDATES) == 0
        return [jnp.where(fresh, s * x[c] + SRC[c, z + M], R[c, z + M]) for c in range(3)]

    engine(
        SWEEPS, FINE, rhs_fine, begin_fine, middle_fine
    )

    def pieces(z, carry):
        for c in range(3):
            v = jnp.where(t < T - 1, X[c, z + N] - XC[c, z + N], X[c, z + N])
            for i in range(PIECES):
                PS[i, c, z] = v[PIECE * i:PIECE * i + PIECE]
        return carry

    lax.fori_loop(0, Z, pieces, 0)
    scatter(PS, CB, csem, "start")

    arrived(CB.at[T - 1], csem.at[1, T - 1])
    for c in range(3):
        JW[c] = jnp.zeros((Z + 2, 8, NX), jnp.float32)
    for c in range(3):
        XW[c] = jnp.zeros((Z + 4, 8, NX), jnp.float32)
        CW[c] = jnp.zeros((Z, 8, NX), jnp.float32)
    for c in range(3):
        XW[c, 2:10, 2:6] = CB[T - 1, c]

    def out_remote(n):
        return remote(PB.at[n], OB.at[me], osem.at[0, n], osem.at[1, me], n, k)

    def emit(n):
        @pl.when(t != n)
        def _():
            out_remote(n).start()

        @pl.when(t == n)
        def _():
            pltpu.make_async_copy(PB.at[n], OB.at[me], osem.at[1, me]).start()

    def halos(n):
        s, r = hsem.at[0, n], hsem.at[1, n]
        return [
            remote(SYU.at[n], YL.at[n, :, 2:10], s.at[0], r.at[0], right, k),
            remote(SYD.at[n], YH.at[n, :, 2:10], s.at[1], r.at[1], left, k),
            remote(PB.at[n, :, 6:8], ZL.at[n], s.at[2], r.at[2], t, up),
            remote(PB.at[n, :, 0:2], ZH.at[n], s.at[3], r.at[3], t, down),
            remote(SYU.at[n, :, 6:8], YL.at[n, :, 0:2], s.at[4], r.at[4], right, up),
            remote(SYU.at[n, :, 0:2], YL.at[n, :, 10:12], s.at[5], r.at[5], right, down),
            remote(SYD.at[n, :, 6:8], YH.at[n, :, 0:2], s.at[6], r.at[6], left, up),
            remote(SYD.at[n, :, 0:2], YH.at[n, :, 10:12], s.at[7], r.at[7], left, down),
        ]

    def propagate(n, carry):
        for c in range(3):
            SYU[n, c] = XW[c, 2:10, 4:6]
            SYD[n, c] = XW[c, 2:10, 2:4]
        emit_first = halos(n)
        for copy in emit_first[4:] + emit_first[:2]:
            copy.start()
        for c in range(3):
            PB[n, c] = XW[c, 2:10, 2:6]
        for copy in emit_first[2:4]:
            copy.start()
        emit(n)
        arrived(JB.at[n], jsem.at[1, n])
        arrived(JC.at[n], ksem.at[1, n])
        for c in range(3):
            JW[c, :, 1:5] = JB[n, c]
            JW[c, :, 5:7] = JC[n, c]
        arrived(CB.at[n], csem.at[1, n])
        for c in range(3):
            CW[c, :, 2:6] = CB[n, c]
        for copy in emit_first:
            copy.wait_recv()
        for c in range(3):
            XW[c, :, 0:2] = YL[n, c]
            XW[c, :, 6:8] = YH[n, c]
            XW[c, 0:2, 2:6] = ZL[n, c]
            XW[c, 10:12, 2:6] = ZH[n, c]
            XW[c, 10:12] = XW[c, 10:12] * keep_top
        x0 = [XW[c] for c in range(3)]
        b = curl([v[:-1] for v in x0], x0[0][1:], x0[1][1:])
        nu = reluctance(b, BW[...], SW[...])
        h = [nu * v for v in b]
        w = step_sizes(MW[...], nu[1:], nu[:-1], RW[...])
        a = curl_adjoint([v[1:] for v in h], h[0][:-1], h[1][:-1])
        x1 = [x0[c][1:-1] + w[c] * (JW[c] - a[c]) for c in range(3)]
        b = curl([v[:-1] for v in x1], x1[0][1:], x1[1][1:])
        h = [nu[1:-1] * v for v in b]
        a = curl_adjoint([v[1:] for v in h], h[0][:-1], h[1][:-1])
        for c in range(3):
            x = x1[c][1:-1]
            drift = MW[1:9] * (x0[c][2:10] - x)
            x = x + w[c][1:-1] * (JW[c, 1:9] + drift - a[c])
            XW[c, 2:10] = x + CW[c]
        return carry

    lax.fori_loop(0, T - 1, propagate, 0)
    for c in range(3):
        PB[T - 1, c] = XW[c, 2:10, 2:6]
    emit(T - 1)

    for i in range(PIECES):
        arrived(OB.at[i], osem.at[1, i])

    def place(z, carry):
        for c in range(3):
            for i in range(PIECES):
                XC[c, z, PIECE * i:PIECE * i + PIECE] = OB[i, c, z]
        return carry

    lax.fori_loop(0, Z, place, 0)
    store = pltpu.make_async_copy(XC.at[:, 0:Z], out, lsem.at[0])
    store.start()

    for copy in first:
        copy.wait_send()

    def sent(m, carry):
        up_copy(m).wait_send()
        down_copy(m).wait_send()
        return carry

    lax.fori_loop(1, FINE - M, sent, 0)
    for u in range(1, (FINE - M - 1) // SWEEPS + 1):
        hz_copy(u).wait_send()
    scatter(PS, CB, csem, "wait_send")

    @pl.when(t < T - 1)
    def _():
        scatter(JS, JB, jsem, "wait_send")
        scatter(JT, JC, ksem, "wait_send")

    def halos_sent(n, carry):
        for copy in halos(n):
            copy.wait_send()
        return carry

    lax.fori_loop(0, T - 1, halos_sent, 0)

    def out_sent(n, carry):
        @pl.when(t != n)
        def _():
            out_remote(n).wait_send()

        return carry

    lax.fori_loop(0, T, out_sent, 0)
    store.wait()


def body(mesh, starts, source, mass_term, curve_entry, curve_table):
    T, K = mesh.shape["tm"], mesh.shape["space"]
    slots = FINE
    f32 = jnp.float32
    vm = lambda *shape: pltpu.VMEM((*shape, NY, NX), f32)
    rows = lambda *shape: pltpu.VMEM(shape, f32)
    dma = lambda *shape: pltpu.SemaphoreType.DMA(shape)
    scratch = [
        vm(3, Z + 2 * N),
        vm(3, Z + 2 * N),
        vm(3, Z + 2 * N),
        vm(3, Z + 2 * M),
        vm(Z + 2 * M),
        pltpu.VMEM((Z, NY, NX), jnp.int32),
        vm(Z + 2 * M + 1),
        vm(Z + 2 * M + 1),
        vm(Z + 2 * M + 1),
        vm(Z + 2 * M + 1),
        vm(3, Z + 2 * M),
        vm(3, Z + 2 * M),
        vm(3, Z + 2 * M),
        vm(slots, 2),
        vm(slots, 2),
        vm(2, STEPS * UPDATES),
        vm(slots, 2),
        vm(slots, 2),
        vm(2, Z + 2 * M),
        vm(2, Z + 2 * M),
        rows(PIECES, 3, Z, PIECE, NX),
        rows(T, 3, Z, PIECE, NX),
        rows(PIECES, 3, Z + 2, 4, NX),
        rows(PIECES, 3, Z + 2, 2, NX),
        rows(T, 3, Z + 2, 4, NX),
        rows(T, 3, Z + 2, 2, NX),
        rows(3, Z + 2, 8, NX),
        rows(T, 3, Z, PIECE, NX),
        rows(T, 3, Z, 2, NX),
        rows(T, 3, Z, 2, NX),
        rows(T, 3, Z + 4, 2, NX),
        rows(T, 3, Z + 4, 2, NX),
        rows(T, 3, 2, PIECE, NX),
        rows(T, 3, 2, PIECE, NX),
        rows(PIECES, 3, Z, PIECE, NX),
        rows(3, Z + 4, 8, NX),
        rows(Z + 2, 8, NX),
        rows(Z + 3, 8, NX),
        rows(Z + 3, 8, NX),
        rows(3, Z, 8, NX),
        rows(Z + 2, 8, NX),
        dma(4), dma(2, 10), dma(2, FINE), dma(2, FINE), dma(2, STEPS * UPDATES),
        dma(2, T), dma(2, T), dma(2, T), dma(2, T, 8), dma(2, T),
    ]
    anywhere = pl.BlockSpec(memory_space=pl.ANY)
    result = pl.pallas_call(
        functools.partial(kernel, T, K),
        out_shape=jax.ShapeDtypeStruct(starts.shape[1:], f32),
        in_specs=[anywhere] * 4 + [pl.BlockSpec(memory_space=pltpu.SMEM)],
        out_specs=anywhere,
        scratch_shapes=scratch,
        compiler_params=pltpu.CompilerParams(
            collective_id=0, has_side_effects=True, vmem_limit_bytes=60 * 1024 * 1024
        ),
    )(starts[0], source[0], mass_term, curve_entry, curve_table)
    return result[None]


def solution(mesh):
    return jax.shard_map(
        functools.partial(body, mesh),
        mesh=mesh,
        in_specs=(
            P("tm", None, "space", None, None),
            P("tm", None, "space", None, None),
            P("space", None, None),
            P("space", None, None),
            P(),
        ),
        out_specs=P("tm", None, "space", None, None),
        check_vma=False,
    )
```

```python
import functools

import jax
import jax.numpy as jnp
from jax import lax
from jax.experimental import pallas as pl
from jax.experimental.pallas import tpu as pltpu
from jax.sharding import PartitionSpec as P

STEPS = 2
UPDATES = 2
SWEEPS = 4
C_SWEEPS = 2
RELAX = 0.45

Z, NY, NX = 8, 32, 128
TBL = 64
PIECE = 4
PIECES = NY // PIECE
PACE = 1
M = 2
N = M + 1
TOP = Z + M - 1
MID = Z // 2 - 1
LAST = MID
FINE = STEPS * UPDATES * SWEEPS


def next_y(v):
    return pltpu.roll(v, v.shape[-2] - 1, v.ndim - 2)


def next_x(v):
    return pltpu.roll(v, v.shape[-1] - 1, v.ndim - 1)


def prev_y(v):
    return pltpu.roll(v, 1, v.ndim - 2)


def prev_x(v):
    return pltpu.roll(v, 1, v.ndim - 1)


def curl_xy(v, above_x, above_y):
    x, y, z = v
    return (next_y(z) - z) - (above_y - y), (above_x - x) - (next_x(z) - z)


def curl_z(v):
    return (next_x(v[1]) - v[1]) - (next_y(v[0]) - v[0])


def curl(v, above_x, above_y):
    return (*curl_xy(v, above_x, above_y), curl_z(v))


def curl_adjoint(h, below_x, below_y):
    x, y, z = h
    return (
        (below_y - y) - (prev_y(z) - z),
        (prev_x(z) - z) - (below_x - x),
        (prev_y(x) - x) - (prev_x(y) - y),
    )


def reluctance(b, base, sat):
    squared = b[0] * b[0] + b[1] * b[1] + b[2] * b[2]
    return base * (1.0 + sat * squared / (1.0 + squared))


def step_sizes(mass, nu, below, relax):
    common = mass + 2.0 * nu
    before_y, before_x = prev_y(nu), prev_x(nu)
    return (
        relax / (common + below + before_y),
        relax / (common + below + before_x),
        relax / (common + before_y + before_x),
    )


def lag(z):
    return MID - z if z <= MID else z - MID - 1


def kernel(
    T, K,
    starts, source, mass, entry, table,
    out,
    X, X0, XC, SRC, S, E, BASE, SAT, NU, NUC, W, WC, R, PQ, V9, HZ, PQS, V9S,
    OLDV, OLDH,
    PS, CB, JS, JT, JB, JC, JW, PB, SYU, SYD, YL, YH, ZL, ZH, OB, XW, MW, BW, SW, CW, RW,
    lsem, isem, psem, vsem, zsem, csem, jsem, ksem, hsem, osem,
):
    t = lax.axis_index("tm")
    k = lax.axis_index("space")
    up, down = lax.rem(k + 1, K), lax.rem(k + K - 1, K)

    def piece_of(d):
        odd = lax.rem(d, 2)
        half = d // 2
        return half * (1 - odd) + (T - 1 - half) * odd

    def group_of(i):
        low = jnp.where(i < T // 2, 1, 0)
        return 2 * i * low + (2 * T - 1 - 2 * i) * (1 - low)

    me = piece_of(t)
    right = group_of(lax.rem(me + 1, T))
    left = group_of(lax.rem(me + T - 1, T))

    def remote(src, dst, send, recv, tm, space):
        return pltpu.make_async_remote_copy(
            src_ref=src, dst_ref=dst, send_sem=send, recv_sem=recv,
            device_id=(tm, space), device_id_type=pl.DeviceIdType.MESH,
        )

    loads = [
        pltpu.make_async_copy(entry, E, lsem.at[3]),
        pltpu.make_async_copy(starts, X0.at[:, N:N + Z], lsem.at[0]),
        pltpu.make_async_copy(source, SRC.at[:, M:M + Z], lsem.at[1]),
        pltpu.make_async_copy(mass, S.at[M:M + Z], lsem.at[2]),
    ]
    for load in loads:
        load.start()

    barrier = pltpu.get_barrier_semaphore()

    def greet(tm, space):
        pl.semaphore_signal(
            barrier, inc=1, device_id=(tm, space), device_id_type=pl.DeviceIdType.MESH
        )

    for space in (up, down):
        for tm in (t, left, right):
            greet(tm, space)
    for r in range(1, T):
        greet(lax.rem(t + r, T), k)

    keep_bottom = jnp.where(k > 0, 1.0, 0.0).astype(jnp.float32)
    keep_top = jnp.where(k < K - 1, 1.0, 0.0).astype(jnp.float32)

    def look_up(lo, hi):
        def plane(p, carry):
            cells = E[p - N]

            def one(j, acc):
                hit = cells == j
                return jnp.where(hit, table[0, j], acc[0]), jnp.where(hit, table[1, j], acc[1])

            zeros = jnp.zeros((NY, NX), jnp.float32)
            b, s = lax.fori_loop(0, TBL, one, (zeros, zeros))
            BASE[p] = b
            SAT[p] = s
            return carry

        lax.fori_loop(lo, hi, plane, 0)

    loads[0].wait()
    look_up(N, N + Z)

    pl.semaphore_wait(barrier, 6 + T - 1)

    first = [
        remote(BASE.at[Z:Z + N], BASE.at[0:N], isem.at[0, 2], isem.at[1, 2], t, up),
        remote(BASE.at[N:N + M], BASE.at[N + Z:], isem.at[0, 3], isem.at[1, 3], t, down),
        remote(SAT.at[Z:Z + N], SAT.at[0:N], isem.at[0, 8], isem.at[1, 8], t, up),
        remote(SAT.at[N:N + M], SAT.at[N + Z:], isem.at[0, 9], isem.at[1, 9], t, down),
        remote(starts.at[:, Z - N:Z], X0.at[:, 0:N], isem.at[0, 0], isem.at[1, 0], t, up),
        remote(starts.at[:, 0:N], X0.at[:, N + Z:], isem.at[0, 1], isem.at[1, 1], t, down),
        remote(mass.at[Z - M:Z], S.at[0:M], isem.at[0, 4], isem.at[1, 4], t, up),
        remote(mass.at[0:M], S.at[M + Z:], isem.at[0, 5], isem.at[1, 5], t, down),
        remote(source.at[:, Z - M:Z], SRC.at[:, 0:M], isem.at[0, 6], isem.at[1, 6], t, up),
        remote(source.at[:, 0:M], SRC.at[:, M + Z:], isem.at[0, 7], isem.at[1, 7], t, down),
    ]
    for copy in first:
        copy.start()

    for load in loads[1:]:
        load.wait()
    for c in range(3):
        X[c, N:N + Z] = X0[c, N:N + Z]

    def scatter(pieces, there, sem, verb):
        for r in range(1, T):
            d = lax.rem(t + r, T)
            copy = remote(pieces.at[piece_of(d)], there.at[t], sem.at[0, r], sem.at[1, t], d, k)
            getattr(copy, verb)()
        if verb == "start":
            pltpu.make_async_copy(pieces.at[me], there.at[t], sem.at[1, t]).start()

    def arrived(ref, sem):
        pltpu.make_async_copy(ref, ref, sem).wait()

    def window_of(v):
        return pltpu.roll(v, lax.rem(2 * NY + 2 - PIECE * me, NY), 0)[0:8]

    def chain_windows():
        for c in range(3):
            def window(p, carry, c=c):
                v = SRC[c, p + M - 1]
                even, odd = pltpu.roll(v, 1, 0), pltpu.roll(v, NY - 3, 0)
                for i in range(PIECES):
                    rows = (odd if i % 2 else even)[8 * (i // 2):8 * (i // 2) + 8]
                    JS[i, c, p] = rows[0:4]
                    JT[i, c, p] = rows[4:6]
                return carry

            lax.fori_loop(0, Z + 2, window, 0)

        @pl.when(t < T - 1)
        def _():
            pltpu.make_async_copy(JS.at[me], JB.at[t], jsem.at[1, t]).start()
            pltpu.make_async_copy(JT.at[me], JC.at[t], ksem.at[1, t]).start()

        for p in range(Z + 3):
            BW[p] = window_of(BASE[p + M - 1])
            SW[p] = window_of(SAT[p + M - 1])
        for p in range(Z + 2):
            MW[p] = window_of(S[p + M - 1]) * (1.0 / STEPS)
            RW[p] = jnp.full((8, NX), RELAX, jnp.float32) * (keep_top if p == Z + 1 else 1.0)

    def field(ref, z):
        return [ref[c, z + N] for c in range(3)]

    def low_parts(v):
        x, y, z = v
        return next_y(z) - z + y, next_x(z) - z + x, curl_z(v)

    def old_coarse():
        def above(ref, z):
            return ref[0, z + N + 1], ref[1, z + N + 1]

        def intensity(ref, z):
            b = curl(field(ref, z), *above(ref, z))
            return [NUC[z + N] * v for v in b]

        for z in range(-2, Z + 1):
            b = curl(field(X0, z), *above(X0, z))
            NUC[z + N] = reluctance(b, BASE[z + N], SAT[z + N])
        for z in range(-1, Z + 1):
            relax = RELAX * keep_top if z >= Z else RELAX
            w = step_sizes(S[z + M] * (1.0 / STEPS), NUC[z + N], NUC[z + N - 1], relax)
            for c in range(3):
                WC[c, z + M] = w[c]
        h = intensity(X0, -2)
        hx, hy = h[0], h[1]
        for z in range(-1, Z + 1):
            h = intensity(X0, z)
            a = curl_adjoint(h, hx, hy)
            for c in range(3):
                XC[c, z + N] = X0[c, z + N] + WC[c, z + M] * (SRC[c, z + M] - a[c])
            hx, hy = h[0], h[1]
        h = intensity(XC, -1)
        hx, hy = h[0], h[1]
        for z in range(Z):
            h = intensity(XC, z)
            a = curl_adjoint(h, hx, hy)
            for c in range(3):
                x = XC[c, z + N]
                drift = (1.0 / STEPS) * S[z + M] * (X0[c, z + N] - x)
                XC[c, z + N] = x + WC[c, z + M] * (SRC[c, z + M] + drift - a[c])
            hx, hy = h[0], h[1]

    def up_copy(slot):
        return remote(PQS.at[slot], PQ.at[slot], psem.at[0, slot], psem.at[1, slot], t, up)

    def hz_copy(u):
        return remote(HZ.at[0, u], HZ.at[1, u], zsem.at[0, u], zsem.at[1, u], t, up)

    def down_copy(slot):
        return remote(V9S.at[slot], V9.at[slot], vsem.at[0, slot], vsem.at[1, slot], t, down)

    def engine(sweeps, total, rhs, begin, middle):
        def plane(a, i, z):
            level = sweeps * a + i - lag(z)
            n, place = (i - lag(z)) // sweeps + a, (i - lag(z)) % sweeps
            active = jnp.logical_and(level >= 0, level < total)
            slot = jnp.clip(level, 0, total - 1)
            is_first = place == 0
            x = field(X, z)
            mass_here = S[z + M]
            if z <= MID:
                if z == -M:
                    low = PQ[slot, 0] - x[1], x[0] - PQ[slot, 1]
                    if is_first:
                        low = (*low, HZ[1, jnp.clip(n, 0, total // sweeps - 1)])
                else:
                    under = field(X, z - 1)
                    low = curl_xy(under, x[0], x[1])
                    if is_first:
                        low = (*low, curl_z(under))
                if is_first:
                    NU[z + N - 1] = reluctance(low, BASE[z + N - 1], SAT[z + N - 1])
                nu_low = NU[z + N - 1]
                hx, hy = nu_low * low[0], nu_low * low[1]
                over = (X[0, z + N + 1], X[1, z + N + 1]) if z == MID else (OLDV[0, z + M + 1], OLDV[1, z + M + 1])
                b = curl(x, *over)
                if z == MID and is_first:
                    NU[z + N] = reluctance(b, BASE[z + N], SAT[z + N])
                if z > -M:
                    OLDV[0, z + M] = x[0]
                    OLDV[1, z + M] = x[1]
            else:
                over = (V9[slot, 0], V9[slot, 1]) if z == TOP else (X[0, z + N + 1], X[1, z + N + 1])
                b = curl(x, *over)
                if is_first:
                    NU[z + N] = reluctance(b, BASE[z + N], SAT[z + N])
                hx, hy = OLDH[0, z + M - 1], OLDH[1, z + M - 1]
            nu = NU[z + N]
            h = [nu * v for v in b]
            if MID <= z < TOP:
                OLDH[0, z + M] = h[0]
                OLDH[1, z + M] = h[1]
            if is_first:
                relax = RELAX * keep_top if z >= Z else RELAX
                w = step_sizes(mass_here, nu, NU[z + N - 1], relax)
                r = rhs(n, z, mass_here, x)
                for c in range(3):
                    W[c, z + M] = w[c]
                    R[c, z + M] = r[c]
            adj = curl_adjoint(h, hx, hy)
            new = []
            for c in range(3):
                v = x[c] + W[c, z + M] * (R[c, z + M] - mass_here * x[c] - adj[c])
                v = jnp.where(active, v, x[c])
                X[c, z + N] = v
                new.append(v)

        def step(a, i):
            s = sweeps * a + i

            @pl.when(s >= LAST + 1)
            def _():
                slot = s - (LAST + M)

                @pl.when(jnp.logical_and(slot >= 1, slot < total - M))
                def _():
                    up_copy(slot).wait_recv()
                    down_copy(slot).wait_recv()
                    if (i - LAST - M) % sweeps == 0:
                        hz_copy(a + (i - LAST - M) // sweeps).wait_recv()

                for z in range(-M, 0):
                    plane(a, i, z)
                for z in range(TOP, Z - 1, -1):
                    plane(a, i, z)

            for z in range(MID):
                plane(a, i, z)
            for z in range(Z - 1, MID + 1, -1):
                plane(a, i, z)
            plane(a, i, MID)
            plane(a, i, MID + 1)

            slot = s + 1 - lag(M)

            @pl.when(jnp.logical_and(slot >= 1, slot < total - M))
            def _():
                V9S[slot, 0] = X[0, M + N]
                V9S[slot, 1] = X[1, M + N]
                down_copy(slot).start()
                low = low_parts(field(X, Z - 1 - M))
                PQS[slot, 0] = low[0]
                PQS[slot, 1] = low[1]
                up_copy(slot).start()
                if (i + 1 - lag(M)) % sweeps == 0:
                    u = a + (i + 1 - lag(M)) // sweeps
                    HZ[0, u] = low[2]
                    hz_copy(u).start()

        steps = total + LAST

        def block(a, carry):
            for i in range(sweeps):
                middle(a, i)
                if i == LAST % sweeps:
                    @pl.when(a == LAST // sweeps)
                    def _():
                        begin()

                if steps % sweeps and i >= steps % sweeps:
                    @pl.when(sweeps * a + i < steps)
                    def _():
                        step(a, i)
                else:
                    step(a, i)
            return carry

        lax.fori_loop(0, (steps + sweeps - 1) // sweeps, block, 0)

    def first_message(slot):
        V9[slot] = X[0:2, N + Z + M]
        low = low_parts(field(X, -N))
        PQ[slot, 0] = low[0]
        PQ[slot, 1] = low[1]
        HZ[1, slot] = low[2]

    def begin_fine():
        for copy in first:
            copy.wait_recv()
        BASE[0:N] = BASE[0:N] * keep_bottom
        for c in range(3):
            X0[c, N + Z:] = X0[c, N + Z:] * keep_top
            X[c, 0:N] = X0[c, 0:N]
            X[c, N + Z:] = X0[c, N + Z:]
        first_message(0)

    def middle_fine(a, i):
        if i == 0:
            @pl.when(jnp.logical_and(a == 2, t < T - 1))
            def _():
                old_coarse()

            @pl.when(a == 1)
            def _():
                chain_windows()

        r = (SWEEPS * a + i - SWEEPS) // PACE + 1

        @pl.when(jnp.logical_and((SWEEPS * a + i) % PACE == 0, jnp.logical_and(t < T - 1, jnp.logical_and(a >= 1, r < T))))
        def _():
            d = lax.rem(t + r, T)
            remote(JS.at[piece_of(d)], JB.at[t], jsem.at[0, r], jsem.at[1, t], d, k).start()
            remote(JT.at[piece_of(d)], JC.at[t], ksem.at[0, r], ksem.at[1, t], d, k).start()

    def rhs_fine(n, z, s, x):
        fresh = lax.rem(n + UPDATES, UPDATES) == 0
        return [jnp.where(fresh, s * x[c] + SRC[c, z + M], R[c, z + M]) for c in range(3)]

    engine(
        SWEEPS, FINE, rhs_fine, begin_fine, middle_fine
    )

    def pieces(z, carry):
        for c in range(3):
            v = jnp.where(t < T - 1, X[c, z + N] - XC[c, z + N], X[c, z + N])
            for i in range(PIECES):
                PS[i, c, z] = v[PIECE * i:PIECE * i + PIECE]
        return carry

    lax.fori_loop(0, Z, pieces, 0)
    urgent = jnp.logical_or(t == 0, t == T - 1)

    @pl.when(urgent)
    def _():
        scatter(PS, CB, csem, "start")


    arrived(CB.at[T - 1], csem.at[1, T - 1])
    for c in range(3):
        JW[c] = jnp.zeros((Z + 2, 8, NX), jnp.float32)
    for c in range(3):
        XW[c] = jnp.zeros((Z + 4, 8, NX), jnp.float32)
        CW[c] = jnp.zeros((Z, 8, NX), jnp.float32)
    for c in range(3):
        XW[c, 2:10, 2:6] = CB[T - 1, c]

    def out_remote(n):
        return remote(PB.at[n], OB.at[me], osem.at[0, n], osem.at[1, me], n, k)

    def emit(n):
        @pl.when(t != n)
        def _():
            out_remote(n).start()

        @pl.when(t == n)
        def _():
            pltpu.make_async_copy(PB.at[n], OB.at[me], osem.at[1, me]).start()

    def halos(n):
        s, r = hsem.at[0, n], hsem.at[1, n]
        return [
            remote(SYU.at[n], YL.at[n, :, 2:10], s.at[0], r.at[0], right, k),
            remote(SYD.at[n], YH.at[n, :, 2:10], s.at[1], r.at[1], left, k),
            remote(PB.at[n, :, 6:8], ZL.at[n], s.at[2], r.at[2], t, up),
            remote(PB.at[n, :, 0:2], ZH.at[n], s.at[3], r.at[3], t, down),
            remote(SYU.at[n, :, 6:8], YL.at[n, :, 0:2], s.at[4], r.at[4], right, up),
            remote(SYU.at[n, :, 0:2], YL.at[n, :, 10:12], s.at[5], r.at[5], right, down),
            remote(SYD.at[n, :, 6:8], YH.at[n, :, 0:2], s.at[6], r.at[6], left, up),
            remote(SYD.at[n, :, 0:2], YH.at[n, :, 10:12], s.at[7], r.at[7], left, down),
        ]

    def propagate(n, carry):
        for c in range(3):
            SYU[n, c] = XW[c, 2:10, 4:6]
            SYD[n, c] = XW[c, 2:10, 2:4]
        emit_first = halos(n)
        for copy in emit_first[4:] + emit_first[:2]:
            copy.start()
        for c in range(3):
            PB[n, c] = XW[c, 2:10, 2:6]
        for copy in emit_first[2:4]:
            copy.start()
        emit(n)

        @pl.when(jnp.logical_and(n == 0, jnp.logical_not(urgent)))
        def _():
            scatter(PS, CB, csem, "start")

        arrived(JB.at[n], jsem.at[1, n])
        arrived(JC.at[n], ksem.at[1, n])
        for c in range(3):
            JW[c, :, 1:5] = JB[n, c]
            JW[c, :, 5:7] = JC[n, c]
        arrived(CB.at[n], csem.at[1, n])
        for c in range(3):
            CW[c, :, 2:6] = CB[n, c]
        for copy in emit_first:
            copy.wait_recv()
        for c in range(3):
            XW[c, :, 0:2] = YL[n, c]
            XW[c, :, 6:8] = YH[n, c]
            XW[c, 0:2, 2:6] = ZL[n, c]
            XW[c, 10:12, 2:6] = ZH[n, c]
            XW[c, 10:12] = XW[c, 10:12] * keep_top
        x0 = [XW[c] for c in range(3)]
        b = curl([v[:-1] for v in x0], x0[0][1:], x0[1][1:])
        nu = reluctance(b, BW[...], SW[...])
        h = [nu * v for v in b]
        w = step_sizes(MW[...], nu[1:], nu[:-1], RW[...])
        a = curl_adjoint([v[1:] for v in h], h[0][:-1], h[1][:-1])
        x1 = [x0[c][1:-1] + w[c] * (JW[c] - a[c]) for c in range(3)]
        b = curl([v[:-1] for v in x1], x1[0][1:], x1[1][1:])
        h = [nu[1:-1] * v for v in b]
        a = curl_adjoint([v[1:] for v in h], h[0][:-1], h[1][:-1])
        for c in range(3):
            x = x1[c][1:-1]
            drift = MW[1:9] * (x0[c][2:10] - x)
            x = x + w[c][1:-1] * (JW[c, 1:9] + drift - a[c])
            XW[c, 2:10] = x + CW[c]
        return carry

    lax.fori_loop(0, T - 1, propagate, 0)
    for c in range(3):
        PB[T - 1, c] = XW[c, 2:10, 2:6]
    emit(T - 1)

    for i in range(PIECES):
        arrived(OB.at[i], osem.at[1, i])

    def place(z, carry):
        for c in range(3):
            for i in range(PIECES):
                XC[c, z, PIECE * i:PIECE * i + PIECE] = OB[i, c, z]
        return carry

    lax.fori_loop(0, Z, place, 0)
    store = pltpu.make_async_copy(XC.at[:, 0:Z], out, lsem.at[0])
    store.start()

    for copy in first:
        copy.wait_send()

    def sent(m, carry):
        up_copy(m).wait_send()
        down_copy(m).wait_send()
        return carry

    lax.fori_loop(1, FINE - M, sent, 0)
    for u in range(1, (FINE - M - 1) // SWEEPS + 1):
        hz_copy(u).wait_send()
    scatter(PS, CB, csem, "wait_send")

    @pl.when(t < T - 1)
    def _():
        scatter(JS, JB, jsem, "wait_send")
        scatter(JT, JC, ksem, "wait_send")

    def halos_sent(n, carry):
        for copy in halos(n):
            copy.wait_send()
        return carry

    lax.fori_loop(0, T - 1, halos_sent, 0)

    def out_sent(n, carry):
        @pl.when(t != n)
        def _():
            out_remote(n).wait_send()

        return carry

    lax.fori_loop(0, T, out_sent, 0)
    store.wait()


def body(mesh, starts, source, mass_term, curve_entry, curve_table):
    T, K = mesh.shape["tm"], mesh.shape["space"]
    slots = FINE
    f32 = jnp.float32
    vm = lambda *shape: pltpu.VMEM((*shape, NY, NX), f32)
    rows = lambda *shape: pltpu.VMEM(shape, f32)
    dma = lambda *shape: pltpu.SemaphoreType.DMA(shape)
    scratch = [
        vm(3, Z + 2 * N),
        vm(3, Z + 2 * N),
        vm(3, Z + 2 * N),
        vm(3, Z + 2 * M),
        vm(Z + 2 * M),
        pltpu.VMEM((Z, NY, NX), jnp.int32),
        vm(Z + 2 * M + 1),
        vm(Z + 2 * M + 1),
        vm(Z + 2 * M + 1),
        vm(Z + 2 * M + 1),
        vm(3, Z + 2 * M),
        vm(3, Z + 2 * M),
        vm(3, Z + 2 * M),
        vm(slots, 2),
        vm(slots, 2),
        vm(2, STEPS * UPDATES),
        vm(slots, 2),
        vm(slots, 2),
        vm(2, Z + 2 * M),
        vm(2, Z + 2 * M),
        rows(PIECES, 3, Z, PIECE, NX),
        rows(T, 3, Z, PIECE, NX),
        rows(PIECES, 3, Z + 2, 4, NX),
        rows(PIECES, 3, Z + 2, 2, NX),
        rows(T, 3, Z + 2, 4, NX),
        rows(T, 3, Z + 2, 2, NX),
        rows(3, Z + 2, 8, NX),
        rows(T, 3, Z, PIECE, NX),
        rows(T, 3, Z, 2, NX),
        rows(T, 3, Z, 2, NX),
        rows(T, 3, Z + 4, 2, NX),
        rows(T, 3, Z + 4, 2, NX),
        rows(T, 3, 2, PIECE, NX),
        rows(T, 3, 2, PIECE, NX),
        rows(PIECES, 3, Z, PIECE, NX),
        rows(3, Z + 4, 8, NX),
        rows(Z + 2, 8, NX),
        rows(Z + 3, 8, NX),
        rows(Z + 3, 8, NX),
        rows(3, Z, 8, NX),
        rows(Z + 2, 8, NX),
        dma(4), dma(2, 10), dma(2, FINE), dma(2, FINE), dma(2, STEPS * UPDATES),
        dma(2, T), dma(2, T), dma(2, T), dma(2, T, 8), dma(2, T),
    ]
    anywhere = pl.BlockSpec(memory_space=pl.ANY)
    result = pl.pallas_call(
        functools.partial(kernel, T, K),
        out_shape=jax.ShapeDtypeStruct(starts.shape[1:], f32),
        in_specs=[anywhere] * 4 + [pl.BlockSpec(memory_space=pltpu.SMEM)],
        out_specs=anywhere,
        scratch_shapes=scratch,
        compiler_params=pltpu.CompilerParams(
            collective_id=0, has_side_effects=True, vmem_limit_bytes=60 * 1024 * 1024
        ),
    )(starts[0], source[0], mass_term, curve_entry, curve_table)
    return result[None]


def solution(mesh):
    return jax.shard_map(
        functools.partial(body, mesh),
        mesh=mesh,
        in_specs=(
            P("tm", None, "space", None, None),
            P("tm", None, "space", None, None),
            P("space", None, None),
            P("space", None, None),
            P(),
        ),
        out_specs=P("tm", None, "space", None, None),
        check_vma=False,
    )
```

```python
import functools

import jax
import jax.numpy as jnp
from jax import lax
from jax.experimental import pallas as pl
from jax.experimental.pallas import tpu as pltpu
from jax.sharding import PartitionSpec as P

STEPS = 2
UPDATES = 2
SWEEPS = 4
C_SWEEPS = 2
RELAX = 0.45

Z, NY, NX = 8, 32, 128
TBL = 64
PIECE = 4
PIECES = NY // PIECE
PACE = 1
M = 2
N = M + 1
TOP = Z + M - 1
MID = Z // 2 - 1
LAST = MID
FINE = STEPS * UPDATES * SWEEPS


def next_y(v):
    return pltpu.roll(v, v.shape[-2] - 1, v.ndim - 2)


def next_x(v):
    return pltpu.roll(v, v.shape[-1] - 1, v.ndim - 1)


def prev_y(v):
    return pltpu.roll(v, 1, v.ndim - 2)


def prev_x(v):
    return pltpu.roll(v, 1, v.ndim - 1)


def curl_xy(v, above_x, above_y):
    x, y, z = v
    return (next_y(z) - z) - (above_y - y), (above_x - x) - (next_x(z) - z)


def curl_z(v):
    return (next_x(v[1]) - v[1]) - (next_y(v[0]) - v[0])


def curl(v, above_x, above_y):
    return (*curl_xy(v, above_x, above_y), curl_z(v))


def curl_adjoint(h, below_x, below_y):
    x, y, z = h
    return (
        (below_y - y) - (prev_y(z) - z),
        (prev_x(z) - z) - (below_x - x),
        (prev_y(x) - x) - (prev_x(y) - y),
    )


def reluctance(b, base, sat):
    squared = b[0] * b[0] + b[1] * b[1] + b[2] * b[2]
    return base * (1.0 + sat * squared / (1.0 + squared))


def step_sizes(mass, nu, below, relax):
    common = mass + 2.0 * nu
    before_y, before_x = prev_y(nu), prev_x(nu)
    return (
        relax / (common + below + before_y),
        relax / (common + below + before_x),
        relax / (common + before_y + before_x),
    )


def lag(z):
    return MID - z if z <= MID else z - MID - 1


def kernel(
    T, K,
    starts, source, mass, entry, table,
    out,
    X, X0, XC, SRC, S, E, BASE, SAT, NU, NUC, W, WC, R, PQ, V9, HZ, PQS, V9S,
    OLDV, OLDH,
    PS, CB, JS, JT, JB, JC, JW, PB, SYU, SYD, YL, YH, ZL, ZH, OB, XW, MW, BW, SW, CW, RW,
    lsem, isem, psem, vsem, zsem, csem, jsem, ksem, hsem, osem,
):
    t = lax.axis_index("tm")
    k = lax.axis_index("space")
    up, down = lax.rem(k + 1, K), lax.rem(k + K - 1, K)

    def piece_of(d):
        odd = lax.rem(d, 2)
        half = d // 2
        return half * (1 - odd) + (T - 1 - half) * odd

    def group_of(i):
        low = jnp.where(i < T // 2, 1, 0)
        return 2 * i * low + (2 * T - 1 - 2 * i) * (1 - low)

    me = piece_of(t)
    right = group_of(lax.rem(me + 1, T))
    left = group_of(lax.rem(me + T - 1, T))

    def remote(src, dst, send, recv, tm, space):
        return pltpu.make_async_remote_copy(
            src_ref=src, dst_ref=dst, send_sem=send, recv_sem=recv,
            device_id=(tm, space), device_id_type=pl.DeviceIdType.MESH,
        )

    loads = [
        pltpu.make_async_copy(entry, E, lsem.at[3]),
        pltpu.make_async_copy(starts, X0.at[:, N:N + Z], lsem.at[0]),
        pltpu.make_async_copy(source, SRC.at[:, M:M + Z], lsem.at[1]),
        pltpu.make_async_copy(mass, S.at[M:M + Z], lsem.at[2]),
    ]
    for load in loads:
        load.start()

    barrier = pltpu.get_barrier_semaphore()

    def greet(tm, space):
        pl.semaphore_signal(
            barrier, inc=1, device_id=(tm, space), device_id_type=pl.DeviceIdType.MESH
        )

    for space in (up, down):
        for tm in (t, left, right):
            greet(tm, space)
    for r in range(1, T):
        greet(lax.rem(t + r, T), k)

    keep_bottom = jnp.where(k > 0, 1.0, 0.0).astype(jnp.float32)
    keep_top = jnp.where(k < K - 1, 1.0, 0.0).astype(jnp.float32)

    def look_up(lo, hi):
        def plane(p, carry):
            cells = E[p - N]

            def one(j, acc):
                hit = cells == j
                return jnp.where(hit, table[0, j], acc[0]), jnp.where(hit, table[1, j], acc[1])

            zeros = jnp.zeros((NY, NX), jnp.float32)
            b, s = lax.fori_loop(0, TBL, one, (zeros, zeros))
            BASE[p] = b
            SAT[p] = s
            return carry

        lax.fori_loop(lo, hi, plane, 0)

    loads[0].wait()
    look_up(N, N + Z)

    pl.semaphore_wait(barrier, 6 + T - 1)

    first = [
        remote(BASE.at[Z:Z + N], BASE.at[0:N], isem.at[0, 2], isem.at[1, 2], t, up),
        remote(BASE.at[N:N + M], BASE.at[N + Z:], isem.at[0, 3], isem.at[1, 3], t, down),
        remote(SAT.at[Z:Z + N], SAT.at[0:N], isem.at[0, 8], isem.at[1, 8], t, up),
        remote(SAT.at[N:N + M], SAT.at[N + Z:], isem.at[0, 9], isem.at[1, 9], t, down),
        remote(starts.at[:, Z - N:Z], X0.at[:, 0:N], isem.at[0, 0], isem.at[1, 0], t, up),
        remote(starts.at[:, 0:N], X0.at[:, N + Z:], isem.at[0, 1], isem.at[1, 1], t, down),
        remote(mass.at[Z - M:Z], S.at[0:M], isem.at[0, 4], isem.at[1, 4], t, up),
        remote(mass.at[0:M], S.at[M + Z:], isem.at[0, 5], isem.at[1, 5], t, down),
        remote(source.at[:, Z - M:Z], SRC.at[:, 0:M], isem.at[0, 6], isem.at[1, 6], t, up),
        remote(source.at[:, 0:M], SRC.at[:, M + Z:], isem.at[0, 7], isem.at[1, 7], t, down),
    ]
    for copy in first:
        copy.start()

    for load in loads[1:]:
        load.wait()
    for c in range(3):
        X[c, N:N + Z] = X0[c, N:N + Z]

    def scatter(pieces, there, sem, verb):
        for r in range(1, T):
            d = lax.rem(t + r, T)
            copy = remote(pieces.at[piece_of(d)], there.at[t], sem.at[0, r], sem.at[1, t], d, k)
            getattr(copy, verb)()
        if verb == "start":
            pltpu.make_async_copy(pieces.at[me], there.at[t], sem.at[1, t]).start()

    def arrived(ref, sem):
        pltpu.make_async_copy(ref, ref, sem).wait()

    def window_of(v):
        return pltpu.roll(v, lax.rem(2 * NY + 2 - PIECE * me, NY), 0)[0:8]

    def chain_windows():
        for c in range(3):
            def window(p, carry, c=c):
                v = SRC[c, p + M - 1]
                even, odd = pltpu.roll(v, 1, 0), pltpu.roll(v, NY - 3, 0)
                for i in range(PIECES):
                    rows = (odd if i % 2 else even)[8 * (i // 2):8 * (i // 2) + 8]
                    JS[i, c, p] = rows[0:4]
                    JT[i, c, p] = rows[4:6]
                return carry

            lax.fori_loop(0, Z + 2, window, 0)

        @pl.when(t < T - 1)
        def _():
            pltpu.make_async_copy(JS.at[me], JB.at[t], jsem.at[1, t]).start()
            pltpu.make_async_copy(JT.at[me], JC.at[t], ksem.at[1, t]).start()

        for p in range(Z + 3):
            BW[p] = window_of(BASE[p + M - 1])
            SW[p] = window_of(SAT[p + M - 1])
        for p in range(Z + 2):
            MW[p] = window_of(S[p + M - 1]) * (1.0 / STEPS)
            RW[p] = jnp.full((8, NX), RELAX, jnp.float32) * (keep_top if p == Z + 1 else 1.0)

    def field(ref, z):
        return [ref[c, z + N] for c in range(3)]

    def low_parts(v):
        x, y, z = v
        return next_y(z) - z + y, next_x(z) - z + x, curl_z(v)

    def old_coarse():
        def above(ref, z):
            return ref[0, z + N + 1], ref[1, z + N + 1]

        def intensity(ref, z):
            b = curl(field(ref, z), *above(ref, z))
            return [NUC[z + N] * v for v in b]

        for z in range(-2, Z + 1):
            b = curl(field(X0, z), *above(X0, z))
            NUC[z + N] = reluctance(b, BASE[z + N], SAT[z + N])
        for z in range(-1, Z + 1):
            relax = RELAX * keep_top if z >= Z else RELAX
            w = step_sizes(S[z + M] * (1.0 / STEPS), NUC[z + N], NUC[z + N - 1], relax)
            for c in range(3):
                WC[c, z + M] = w[c]
        h = intensity(X0, -2)
        hx, hy = h[0], h[1]
        for z in range(-1, Z + 1):
            h = intensity(X0, z)
            a = curl_adjoint(h, hx, hy)
            for c in range(3):
                XC[c, z + N] = X0[c, z + N] + WC[c, z + M] * (SRC[c, z + M] - a[c])
            hx, hy = h[0], h[1]
        h = intensity(XC, -1)
        hx, hy = h[0], h[1]
        for z in range(Z):
            h = intensity(XC, z)
            a = curl_adjoint(h, hx, hy)
            for c in range(3):
                x = XC[c, z + N]
                drift = (1.0 / STEPS) * S[z + M] * (X0[c, z + N] - x)
                XC[c, z + N] = x + WC[c, z + M] * (SRC[c, z + M] + drift - a[c])
            hx, hy = h[0], h[1]

    def up_copy(slot):
        return remote(PQS.at[slot], PQ.at[slot], psem.at[0, slot], psem.at[1, slot], t, up)

    def hz_copy(u):
        return remote(HZ.at[0, u], HZ.at[1, u], zsem.at[0, u], zsem.at[1, u], t, up)

    def down_copy(slot):
        return remote(V9S.at[slot], V9.at[slot], vsem.at[0, slot], vsem.at[1, slot], t, down)

    def engine(sweeps, total, rhs, begin, middle):
        def plane(a, i, z):
            level = sweeps * a + i - lag(z)
            n, place = (i - lag(z)) // sweeps + a, (i - lag(z)) % sweeps
            active = jnp.logical_and(level >= 0, level < total)
            slot = jnp.clip(level, 0, total - 1)
            is_first = place == 0
            x = field(X, z)
            mass_here = S[z + M]
            if z <= MID:
                if z == -M:
                    low = PQ[slot, 0] - x[1], x[0] - PQ[slot, 1]
                    if is_first:
                        low = (*low, HZ[1, jnp.clip(n, 0, total // sweeps - 1)])
                else:
                    under = field(X, z - 1)
                    low = curl_xy(under, x[0], x[1])
                    if is_first:
                        low = (*low, curl_z(under))
                if is_first:
                    NU[z + N - 1] = reluctance(low, BASE[z + N - 1], SAT[z + N - 1])
                nu_low = NU[z + N - 1]
                hx, hy = nu_low * low[0], nu_low * low[1]
                over = (X[0, z + N + 1], X[1, z + N + 1]) if z == MID else (OLDV[0, z + M + 1], OLDV[1, z + M + 1])
                b = curl(x, *over)
                if z == MID and is_first:
                    NU[z + N] = reluctance(b, BASE[z + N], SAT[z + N])
                if z > -M:
                    OLDV[0, z + M] = x[0]
                    OLDV[1, z + M] = x[1]
            else:
                over = (V9[slot, 0], V9[slot, 1]) if z == TOP else (X[0, z + N + 1], X[1, z + N + 1])
                b = curl(x, *over)
                if is_first:
                    NU[z + N] = reluctance(b, BASE[z + N], SAT[z + N])
                hx, hy = OLDH[0, z + M - 1], OLDH[1, z + M - 1]
            nu = NU[z + N]
            h = [nu * v for v in b]
            if MID <= z < TOP:
                OLDH[0, z + M] = h[0]
                OLDH[1, z + M] = h[1]
            if is_first:
                relax = RELAX * keep_top if z >= Z else RELAX
                w = step_sizes(mass_here, nu, NU[z + N - 1], relax)
                r = rhs(n, z, mass_here, x)
                for c in range(3):
                    W[c, z + M] = w[c]
                    R[c, z + M] = r[c]
            adj = curl_adjoint(h, hx, hy)
            new = []
            for c in range(3):
                v = x[c] + W[c, z + M] * (R[c, z + M] - mass_here * x[c] - adj[c])
                v = jnp.where(active, v, x[c])
                X[c, z + N] = v
                new.append(v)

        def step(a, i):
            s = sweeps * a + i

            @pl.when(s >= LAST + 1)
            def _():
                slot = s - (LAST + M)

                @pl.when(jnp.logical_and(slot >= 1, slot < total - M))
                def _():
                    up_copy(slot).wait_recv()
                    down_copy(slot).wait_recv()
                    if (i - LAST - M) % sweeps == 0:
                        hz_copy(a + (i - LAST - M) // sweeps).wait_recv()

                for z in range(-M, 0):
                    plane(a, i, z)
                for z in range(TOP, Z - 1, -1):
                    plane(a, i, z)

            for z in range(MID):
                plane(a, i, z)
            for z in range(Z - 1, MID + 1, -1):
                plane(a, i, z)
            plane(a, i, MID)
            plane(a, i, MID + 1)

            slot = s + 1 - lag(M)

            @pl.when(jnp.logical_and(slot >= 1, slot < total - M))
            def _():
                V9S[slot, 0] = X[0, M + N]
                V9S[slot, 1] = X[1, M + N]
                down_copy(slot).start()
                low = low_parts(field(X, Z - 1 - M))
                PQS[slot, 0] = low[0]
                PQS[slot, 1] = low[1]
                up_copy(slot).start()
                if (i + 1 - lag(M)) % sweeps == 0:
                    u = a + (i + 1 - lag(M)) // sweeps
                    HZ[0, u] = low[2]
                    hz_copy(u).start()

        steps = total + LAST

        def block(a, carry):
            for i in range(sweeps):
                middle(a, i)
                if i == LAST % sweeps:
                    @pl.when(a == LAST // sweeps)
                    def _():
                        begin()

                if steps % sweeps and i >= steps % sweeps:
                    @pl.when(sweeps * a + i < steps)
                    def _():
                        step(a, i)
                else:
                    step(a, i)
            return carry

        lax.fori_loop(0, (steps + sweeps - 1) // sweeps, block, 0)

    def first_message(slot):
        V9[slot] = X[0:2, N + Z + M]
        low = low_parts(field(X, -N))
        PQ[slot, 0] = low[0]
        PQ[slot, 1] = low[1]
        HZ[1, slot] = low[2]

    def begin_fine():
        for copy in first:
            copy.wait_recv()
        BASE[0:N] = BASE[0:N] * keep_bottom
        for c in range(3):
            X0[c, N + Z:] = X0[c, N + Z:] * keep_top
            X[c, 0:N] = X0[c, 0:N]
            X[c, N + Z:] = X0[c, N + Z:]
        first_message(0)

    def middle_fine(a, i):
        if i == 0:
            @pl.when(jnp.logical_and(a == 2, t < T - 1))
            def _():
                old_coarse()

            @pl.when(a == 1)
            def _():
                chain_windows()

        r = (SWEEPS * a + i - SWEEPS) // PACE + 1

        @pl.when(jnp.logical_and((SWEEPS * a + i) % PACE == 0, jnp.logical_and(t < T - 1, jnp.logical_and(a >= 1, r < T))))
        def _():
            d = lax.rem(t + r, T)
            remote(JS.at[piece_of(d)], JB.at[t], jsem.at[0, r], jsem.at[1, t], d, k).start()
            remote(JT.at[piece_of(d)], JC.at[t], ksem.at[0, r], ksem.at[1, t], d, k).start()

    def rhs_fine(n, z, s, x):
        fresh = lax.rem(n + UPDATES, UPDATES) == 0
        return [jnp.where(fresh, s * x[c] + SRC[c, z + M], R[c, z + M]) for c in range(3)]

    engine(
        SWEEPS, FINE, rhs_fine, begin_fine, middle_fine
    )

    def pieces(z, carry):
        for c in range(3):
            v = jnp.where(t < T - 1, X[c, z + N] - XC[c, z + N], X[c, z + N])
            for i in range(PIECES):
                PS[i, c, z] = v[PIECE * i:PIECE * i + PIECE]
        return carry

    lax.fori_loop(0, Z, pieces, 0)
    urgent = jnp.logical_or(t == 0, t == T - 1)

    @pl.when(urgent)
    def _():
        scatter(PS, CB, csem, "start")


    arrived(CB.at[T - 1], csem.at[1, T - 1])
    for c in range(3):
        JW[c] = jnp.zeros((Z + 2, 8, NX), jnp.float32)
    for c in range(3):
        XW[c] = jnp.zeros((Z + 4, 8, NX), jnp.float32)
        CW[c] = jnp.zeros((Z, 8, NX), jnp.float32)
    for c in range(3):
        XW[c, 2:10, 2:6] = CB[T - 1, c]

    def out_remote(n):
        return remote(PB.at[n], OB.at[me], osem.at[0, n], osem.at[1, me], n, k)

    def emit(n):
        @pl.when(t != n)
        def _():
            out_remote(n).start()

        @pl.when(t == n)
        def _():
            pltpu.make_async_copy(PB.at[n], OB.at[me], osem.at[1, me]).start()

    def halos(n):
        s, r = hsem.at[0, n], hsem.at[1, n]
        return [
            remote(SYU.at[n], YL.at[n, :, 2:10], s.at[0], r.at[0], right, k),
            remote(SYD.at[n], YH.at[n, :, 2:10], s.at[1], r.at[1], left, k),
            remote(PB.at[n, :, 6:8], ZL.at[n], s.at[2], r.at[2], t, up),
            remote(PB.at[n, :, 0:2], ZH.at[n], s.at[3], r.at[3], t, down),
            remote(SYU.at[n, :, 6:8], YL.at[n, :, 0:2], s.at[4], r.at[4], right, up),
            remote(SYU.at[n, :, 0:2], YL.at[n, :, 10:12], s.at[5], r.at[5], right, down),
            remote(SYD.at[n, :, 6:8], YH.at[n, :, 0:2], s.at[6], r.at[6], left, up),
            remote(SYD.at[n, :, 0:2], YH.at[n, :, 10:12], s.at[7], r.at[7], left, down),
        ]

    def propagate(n, carry):
        for c in range(3):
            SYU[n, c] = XW[c, 2:10, 4:6]
            SYD[n, c] = XW[c, 2:10, 2:4]
        emit_first = halos(n)
        for copy in emit_first[4:] + emit_first[:2]:
            copy.start()
        for c in range(3):
            PB[n, c] = XW[c, 2:10, 2:6]
        for copy in emit_first[2:4]:
            copy.start()
        emit(n)

        @pl.when(jnp.logical_and(n == (t >= 4).astype(jnp.int32), jnp.logical_not(urgent)))
        def _():
            scatter(PS, CB, csem, "start")

        arrived(JB.at[n], jsem.at[1, n])
        arrived(JC.at[n], ksem.at[1, n])
        for c in range(3):
            JW[c, :, 1:5] = JB[n, c]
            JW[c, :, 5:7] = JC[n, c]
        arrived(CB.at[n], csem.at[1, n])
        for c in range(3):
            CW[c, :, 2:6] = CB[n, c]
        for copy in emit_first:
            copy.wait_recv()
        for c in range(3):
            XW[c, :, 0:2] = YL[n, c]
            XW[c, :, 6:8] = YH[n, c]
            XW[c, 0:2, 2:6] = ZL[n, c]
            XW[c, 10:12, 2:6] = ZH[n, c]
            XW[c, 10:12] = XW[c, 10:12] * keep_top
        x0 = [XW[c] for c in range(3)]
        b = curl([v[:-1] for v in x0], x0[0][1:], x0[1][1:])
        nu = reluctance(b, BW[...], SW[...])
        h = [nu * v for v in b]
        w = step_sizes(MW[...], nu[1:], nu[:-1], RW[...])
        a = curl_adjoint([v[1:] for v in h], h[0][:-1], h[1][:-1])
        x1 = [x0[c][1:-1] + w[c] * (JW[c] - a[c]) for c in range(3)]
        b = curl([v[:-1] for v in x1], x1[0][1:], x1[1][1:])
        h = [nu[1:-1] * v for v in b]
        a = curl_adjoint([v[1:] for v in h], h[0][:-1], h[1][:-1])
        for c in range(3):
            x = x1[c][1:-1]
            drift = MW[1:9] * (x0[c][2:10] - x)
            x = x + w[c][1:-1] * (JW[c, 1:9] + drift - a[c])
            XW[c, 2:10] = x + CW[c]
        return carry

    lax.fori_loop(0, T - 1, propagate, 0)
    for c in range(3):
        PB[T - 1, c] = XW[c, 2:10, 2:6]
    emit(T - 1)

    for i in range(PIECES):
        arrived(OB.at[i], osem.at[1, i])

    def place(z, carry):
        for c in range(3):
            for i in range(PIECES):
                XC[c, z, PIECE * i:PIECE * i + PIECE] = OB[i, c, z]
        return carry

    lax.fori_loop(0, Z, place, 0)
    store = pltpu.make_async_copy(XC.at[:, 0:Z], out, lsem.at[0])
    store.start()

    for copy in first:
        copy.wait_send()

    def sent(m, carry):
        up_copy(m).wait_send()
        down_copy(m).wait_send()
        return carry

    lax.fori_loop(1, FINE - M, sent, 0)
    for u in range(1, (FINE - M - 1) // SWEEPS + 1):
        hz_copy(u).wait_send()
    scatter(PS, CB, csem, "wait_send")

    @pl.when(t < T - 1)
    def _():
        scatter(JS, JB, jsem, "wait_send")
        scatter(JT, JC, ksem, "wait_send")

    def halos_sent(n, carry):
        for copy in halos(n):
            copy.wait_send()
        return carry

    lax.fori_loop(0, T - 1, halos_sent, 0)

    def out_sent(n, carry):
        @pl.when(t != n)
        def _():
            out_remote(n).wait_send()

        return carry

    lax.fori_loop(0, T, out_sent, 0)
    store.wait()


def body(mesh, starts, source, mass_term, curve_entry, curve_table):
    T, K = mesh.shape["tm"], mesh.shape["space"]
    slots = FINE
    f32 = jnp.float32
    vm = lambda *shape: pltpu.VMEM((*shape, NY, NX), f32)
    rows = lambda *shape: pltpu.VMEM(shape, f32)
    dma = lambda *shape: pltpu.SemaphoreType.DMA(shape)
    scratch = [
        vm(3, Z + 2 * N),
        vm(3, Z + 2 * N),
        vm(3, Z + 2 * N),
        vm(3, Z + 2 * M),
        vm(Z + 2 * M),
        pltpu.VMEM((Z, NY, NX), jnp.int32),
        vm(Z + 2 * M + 1),
        vm(Z + 2 * M + 1),
        vm(Z + 2 * M + 1),
        vm(Z + 2 * M + 1),
        vm(3, Z + 2 * M),
        vm(3, Z + 2 * M),
        vm(3, Z + 2 * M),
        vm(slots, 2),
        vm(slots, 2),
        vm(2, STEPS * UPDATES),
        vm(slots, 2),
        vm(slots, 2),
        vm(2, Z + 2 * M),
        vm(2, Z + 2 * M),
        rows(PIECES, 3, Z, PIECE, NX),
        rows(T, 3, Z, PIECE, NX),
        rows(PIECES, 3, Z + 2, 4, NX),
        rows(PIECES, 3, Z + 2, 2, NX),
        rows(T, 3, Z + 2, 4, NX),
        rows(T, 3, Z + 2, 2, NX),
        rows(3, Z + 2, 8, NX),
        rows(T, 3, Z, PIECE, NX),
        rows(T, 3, Z, 2, NX),
        rows(T, 3, Z, 2, NX),
        rows(T, 3, Z + 4, 2, NX),
        rows(T, 3, Z + 4, 2, NX),
        rows(T, 3, 2, PIECE, NX),
        rows(T, 3, 2, PIECE, NX),
        rows(PIECES, 3, Z, PIECE, NX),
        rows(3, Z + 4, 8, NX),
        rows(Z + 2, 8, NX),
        rows(Z + 3, 8, NX),
        rows(Z + 3, 8, NX),
        rows(3, Z, 8, NX),
        rows(Z + 2, 8, NX),
        dma(4), dma(2, 10), dma(2, FINE), dma(2, FINE), dma(2, STEPS * UPDATES),
        dma(2, T), dma(2, T), dma(2, T), dma(2, T, 8), dma(2, T),
    ]
    anywhere = pl.BlockSpec(memory_space=pl.ANY)
    result = pl.pallas_call(
        functools.partial(kernel, T, K),
        out_shape=jax.ShapeDtypeStruct(starts.shape[1:], f32),
        in_specs=[anywhere] * 4 + [pl.BlockSpec(memory_space=pltpu.SMEM)],
        out_specs=anywhere,
        scratch_shapes=scratch,
        compiler_params=pltpu.CompilerParams(
            collective_id=0, has_side_effects=True, vmem_limit_bytes=60 * 1024 * 1024
        ),
    )(starts[0], source[0], mass_term, curve_entry, curve_table)
    return result[None]


def solution(mesh):
    return jax.shard_map(
        functools.partial(body, mesh),
        mesh=mesh,
        in_specs=(
            P("tm", None, "space", None, None),
            P("tm", None, "space", None, None),
            P("space", None, None),
            P("space", None, None),
            P(),
        ),
        out_specs=P("tm", None, "space", None, None),
        check_vma=False,
    )
```
